128 devices in a mesh: row: 16 (over y_lo, z, core), col: 8 (over x, y_hi).
Axes of the slice: x: 4, y: 4 (y_hi: 2, y_lo: 2; y = y_hi * 2 + y_lo), z: 4, core: 2. Of those that a mesh axis runs over, the one named last changes fastest.
Arguments:
- pair: float32 [1024, 1024, 128], P('row', 'col'), may hold values from -6 to 6
- ln_gain: float32 [128], replicated, may hold values from 0.1 to 1.9
- ln_bias: float32 [128], replicated, may hold values from -3 to 3
- w_left: bfloat16 [128, 256], replicated, may hold values from -0.5 to 0.5
- w_right: bfloat16 [128, 256], replicated, may hold values from -0.5 to 0.5
- w_gate: bfloat16 [128, 128], replicated, may hold values from -0.5 to 0.5
- w_out: bfloat16 [128, 128], replicated, may hold values from -0.5 to 0.5
- out_gain: float32 [128], replicated, may hold values from 0.1 to 1.9
- out_bias: float32 [128], replicated, may hold values from -3 to 3
Outputs:
- update: float32 [1024, 1024, 128], P('row', 'col')
The draws below stay inside these ranges and needn't reach their ends.
All inputs are finite; a program needn't handle non-finite values.
Results may differ from the reference program's by a relative error of at most 0.018.
Values may be sent and summed in bfloat16 or wider, within the bound.
No kernel may reach another device: no remote copies, remote signals or barrier semaphores. Data moves between devices by JAX's collectives and lax.ppermute only.
A program may use at most 320 MiB of HBM per device.

```python
import jax
import jax.numpy as jnp
from jax import lax

C = 128
CH = 128
N = 1024


def block_scale(key, dims, pieces, smallest, top_value):
    level, own = 1.0, jax.random.fold_in(key, 6)
    for dim, parts in pieces:
        heights = jnp.exp(jax.random.uniform(jax.random.fold_in(own, dim), (parts,), jnp.float32, smallest / len(pieces), top_value / len(pieces)))
        level = level * jnp.repeat(heights, dims[dim] // parts).reshape([-1 if axis == dim else 1 for axis in range(len(dims))])
    return level


def centred(key, extent, deviation, reach, split=(), dtype=jnp.bfloat16):
    array = deviation * jax.random.normal(key, extent, jnp.float32)
    if split:
        array = array * block_scale(key, extent, split, -0.22, 0.18)
    return jnp.clip(array, -reach, reach).astype(dtype)


def setup_inputs(seed: int = 0) -> dict:
    splits = jax.random.split(jax.random.key(seed), 10)
    pair = centred(splits[0], (N, N, C), 1.0, 6.0, ((0, 16), (1, 8)), jnp.float32)
    ln_gain = jnp.clip(1.0 + 0.18 * jax.random.normal(splits[1], (C,), jnp.float32), 0.1, 1.9)
    ln_bias = centred(splits[2], (C,), 0.5, 3.0, (), jnp.float32)
    w_left = centred(splits[3], (C, 2 * CH), C ** -0.5, 0.5)
    w_right = centred(splits[4], (C, 2 * CH), C ** -0.5, 0.5)
    w_gate = centred(splits[5], (C, C), C ** -0.5, 0.5)
    w_out = centred(splits[6], (CH, C), CH ** -0.5, 0.5)
    out_gain = jnp.clip(1.0 + 0.18 * jax.random.normal(splits[7], (CH,), jnp.float32), 0.1, 1.9)
    out_bias = centred(splits[8], (CH,), 0.5, 3.0, (), jnp.float32)
    return dict(pair=pair, ln_gain=ln_gain, ln_bias=ln_bias, w_left=w_left, w_right=w_right, w_gate=w_gate, w_out=w_out, out_gain=out_gain, out_bias=out_bias)


def layer_norm(values, gain, bias):
    center = lax.optimization_barrier(jnp.mean(values, axis=-1, keepdims=True))
    spread = lax.optimization_barrier(jnp.mean((values - center) ** 2, axis=-1, keepdims=True))
    return (values - center) * lax.rsqrt(spread + 1e-05) * gain + bias

def gated_edges(normed, weight):
    half = weight.shape[1] // 2
    projected = jnp.dot(normed, weight, preferred_element_type=jnp.float32)
    return (jax.nn.sigmoid(projected[..., :half]) * projected[..., half:]).astype(jnp.bfloat16)

def channel_product(operands):
    return jnp.dot(operands[0].T, operands[1], preferred_element_type=jnp.float32)

def reference(pair, ln_gain, ln_bias, w_left, w_right, w_gate, w_out, out_gain, out_bias):
    normed = layer_norm(pair, ln_gain, ln_bias).astype(jnp.bfloat16)
    left_edges = gated_edges(normed, w_left)
    right_edges = gated_edges(normed, w_right)
    gating = jax.nn.sigmoid(jnp.dot(normed, w_gate, preferred_element_type=jnp.float32))
    left_major = jnp.moveaxis(left_edges, 2, 0)
    right_major = jnp.moveaxis(right_edges, 2, 0)
    product = jnp.moveaxis(lax.map(channel_product, (left_major, right_major)), 0, 2)
    product_normed = layer_norm(product, out_gain, out_bias).astype(jnp.bfloat16)
    return gating * jnp.dot(product_normed, w_out, preferred_element_type=jnp.float32)
```

```python
import jax
import jax.numpy as jnp
from jax import lax
from jax.experimental import pallas as pl
from jax.experimental.pallas import tpu as pltpu
from jax.sharding import PartitionSpec as P

F32, BF16 = jnp.float32, jnp.bfloat16
EPS = 1e-05
ROWS = 16
VMEM = 48 * 2**20


def sigmoid(values):
    return 0.5 * jnp.tanh(0.5 * values) + 0.5


def normalize(values, gain, bias):
    center = jnp.mean(values, axis=-1, keepdims=True)
    values = values - center
    spread = jnp.mean(values * values, axis=-1, keepdims=True)
    return (values * lax.rsqrt(spread + EPS) * gain + bias).astype(BF16)


def edges_kernel(pair, gain, bias, weight, left, right, left_rows, right_rows):
    rows, tokens, channels = pair.shape
    for row in range(0, rows, 2):
        normed = normalize(pair[row : row + 2].reshape(2 * tokens, channels), gain[...], bias[...])
        projected = lax.dot_general(
            weight[...], normed, (((1,), (1,)), ((), ())), preferred_element_type=F32
        )
        lefts = sigmoid(projected[:channels]) * projected[channels : 2 * channels]
        rights = sigmoid(projected[2 * channels : 3 * channels]) * projected[3 * channels :]
        for half in range(2):
            place = pl.ds((row + half) * channels, channels)
            lanes = slice(half * tokens, (half + 1) * tokens)
            left_rows[place, :] = lefts[:, lanes]
            right_rows[place, :] = rights[:, lanes]
    for channel in range(channels):
        left[channel] = left_rows[pl.ds(channel, rows, stride=channels), :].astype(BF16)
        right[channel] = right_rows[pl.ds(channel, rows, stride=channels), :].astype(BF16)


def edges(pair, gain, bias, weight):
    rows, tokens, channels = pair.shape
    whole = lambda *shape: pl.BlockSpec(shape, lambda step: (0,) * len(shape))
    out = pl.BlockSpec((channels, ROWS, tokens), lambda step: (0, step, 0))
    return pl.pallas_call(
        edges_kernel,
        grid=(rows // ROWS,),
        in_specs=[
            pl.BlockSpec((ROWS, tokens, channels), lambda step: (step, 0, 0)),
            whole(1, channels),
            whole(1, channels),
            whole(4 * channels, channels),
        ],
        out_specs=[out, out],
        out_shape=[jax.ShapeDtypeStruct((channels, rows, tokens), BF16)] * 2,
        scratch_shapes=[pltpu.VMEM((ROWS * channels, tokens), F32)] * 2,
        compiler_params=pltpu.CompilerParams(vmem_limit_bytes=VMEM),
        cost_estimate=pl.CostEstimate(
            flops=8 * rows * tokens * channels * channels,
            bytes_accessed=8 * rows * tokens * channels,
            transcendentals=2 * rows * tokens * channels,
        ),
        name="edges",
    )(pair, gain, bias, weight)


def gating_kernel(pair, gain, bias, weight, gating):
    rows, tokens, channels = pair.shape
    normed = normalize(pair[...].reshape(rows * tokens, channels), gain[...], bias[...])
    projected = jnp.dot(normed, weight[...], preferred_element_type=F32)
    gating[...] = sigmoid(projected).reshape(rows, tokens, channels)


def gates(pair, gain, bias, weight):
    rows, tokens, channels = pair.shape
    whole = lambda *shape: pl.BlockSpec(shape, lambda step: (0,) * len(shape))
    block = pl.BlockSpec((ROWS, tokens, channels), lambda step: (step, 0, 0))
    return pl.pallas_call(
        gating_kernel,
        grid=(rows // ROWS,),
        in_specs=[block, whole(1, channels), whole(1, channels), whole(channels, channels)],
        out_specs=block,
        out_shape=jax.ShapeDtypeStruct(pair.shape, F32),
        compiler_params=pltpu.CompilerParams(vmem_limit_bytes=VMEM),
        cost_estimate=pl.CostEstimate(
            flops=2 * rows * tokens * channels * channels,
            bytes_accessed=8 * rows * tokens * channels,
            transcendentals=rows * tokens * channels,
        ),
        name="gates",
    )(pair, gain, bias, weight)


def product_kernel(left, right, out, left_turned, right_whole):
    n_rows, n_cols, depth, tokens = left.shape
    for col in range(n_cols):
        lanes = slice(col * tokens, (col + 1) * tokens)
        for row in range(n_rows):
            right_whole[row * depth : (row + 1) * depth, lanes] = right[row, col]
        column = jnp.concatenate([left[row, col] for row in range(n_rows)], axis=0)
        left_turned[lanes, :] = column.T
    wide = 2 * tokens
    for start in range(0, n_cols * tokens, wide):
        total = jnp.dot(
            left_turned[...], right_whole[:, start : start + wide], preferred_element_type=F32
        ).astype(BF16)
        for part in range(2):
            block = total[:, part * tokens : (part + 1) * tokens]
            out[:, start // tokens + part] = block.reshape(n_rows, depth, tokens)


def products(left, right):
    n_rows, n_cols, depth, tokens = left.shape
    size = n_rows * depth
    return pl.pallas_call(
        product_kernel,
        out_shape=jax.ShapeDtypeStruct(left.shape, BF16),
        scratch_shapes=[pltpu.VMEM((size, size), BF16)] * 2,
        compiler_params=pltpu.CompilerParams(vmem_limit_bytes=VMEM),
        cost_estimate=pl.CostEstimate(
            flops=2 * size**3, bytes_accessed=6 * size * size, transcendentals=0
        ),
        name="products",
    )(left, right)


def update_kernel(product, gating, gain, bias, weight, out, rows_of):
    channels, rows, tokens = product.shape
    values = product[...].astype(F32)
    center = jnp.sum(values, axis=0, keepdims=True) * (1.0 / channels)
    values = values - center
    spread = jnp.sum(values * values, axis=0, keepdims=True) * (1.0 / channels)
    values = values * lax.rsqrt(spread + EPS) * gain[...] + bias[...]
    rows_of[...] = values.reshape(channels * rows, tokens)
    for row in range(rows):
        normed = rows_of[pl.ds(row, channels, stride=rows), :].astype(BF16)
        projected = lax.dot_general(
            normed, weight[...], (((0,), (0,)), ((), ())), preferred_element_type=F32
        )
        out[row] = gating[row] * projected


def update(product, gating, gain, bias, weight):
    channels, rows, tokens = product.shape
    whole = lambda *shape: pl.BlockSpec(shape, lambda step: (0,) * len(shape))
    block = pl.BlockSpec((ROWS, tokens, channels), lambda step: (step, 0, 0))
    spread = lambda vector: jnp.broadcast_to(vector[:, None, None], (channels, 1, tokens))
    return pl.pallas_call(
        update_kernel,
        grid=(rows // ROWS,),
        in_specs=[
            pl.BlockSpec((channels, ROWS, tokens), lambda step: (0, step, 0)),
            block,
            whole(channels, 1, tokens),
            whole(channels, 1, tokens),
            whole(channels, channels),
        ],
        out_specs=block,
        out_shape=jax.ShapeDtypeStruct((rows, tokens, channels), F32),
        scratch_shapes=[pltpu.VMEM((channels * ROWS, tokens), F32)],
        compiler_params=pltpu.CompilerParams(vmem_limit_bytes=VMEM),
        cost_estimate=pl.CostEstimate(
            flops=2 * rows * tokens * channels * channels,
            bytes_accessed=10 * rows * tokens * channels,
            transcendentals=0,
        ),
        name="update",
    )(product, gating, spread(gain), spread(bias), weight)


def per_device(n_rows, n_cols, pair, ln_gain, ln_bias, w_left, w_right, w_gate, w_out, out_gain, out_bias):
    rows, tokens, channels = pair.shape
    axes = ("row", "col")
    gain, bias = ln_gain[None], ln_bias[None]
    weight = jnp.concatenate([w_left.T, w_right.T], axis=0)
    left, right = edges(pair, gain, bias, weight)
    gating = gates(pair, gain, bias, w_gate)
    grid = (n_rows, n_cols, rows, tokens)
    left = lax.all_to_all(left, axes, 0, 0, tiled=True).reshape(grid)
    right = lax.all_to_all(right, axes, 0, 0, tiled=True).reshape(grid)
    product = products(left, right).reshape(channels, rows, tokens)
    product = lax.all_to_all(product, axes, 0, 0, tiled=True)
    return update(product, gating, out_gain, out_bias, w_out)


def solution(mesh):
    n_rows, n_cols = mesh.shape["row"], mesh.shape["col"]
    return jax.shard_map(
        lambda *args: per_device(n_rows, n_cols, *args),
        mesh=mesh,
        in_specs=(P("row", "col", None), P(), P(), P(), P(), P(), P(), P(), P()),
        out_specs=P("row", "col", None),
        check_vma=False,
    )
```

```python
import jax
import jax.numpy as jnp
from jax import lax
from jax.experimental import pallas as pl
from jax.experimental.pallas import tpu as pltpu
from jax.sharding import PartitionSpec as P

F32, BF16 = jnp.float32, jnp.bfloat16
EPS = 1e-05
ROWS = 16
PAD = 4


def sigmoid(values):
    return 0.5 * jnp.tanh(0.5 * values) + 0.5


def normalize(values, gain, bias):
    center = jnp.mean(values, axis=-1, keepdims=True)
    values = values - center
    spread = jnp.mean(values * values, axis=-1, keepdims=True)
    return (values * lax.rsqrt(spread + EPS) * gain + bias).astype(BF16)


def edges_kernel(pair, gain, bias, w_left, w_right, out, weight, left_rows, right_rows):
    rows, tokens, channels = pair.shape
    pitch = channels + PAD

    @pl.when(pl.program_id(0) == 0)
    def _():
        weight[: 2 * channels] = w_left[...].T
        weight[2 * channels :] = w_right[...].T

    for row in range(0, rows, 2):
        normed = normalize(pair[row : row + 2].reshape(2 * tokens, channels), gain[...], bias[...])
        projected = lax.dot_general(
            weight[...], normed, (((1,), (1,)), ((), ())), preferred_element_type=F32
        )
        lefts = sigmoid(projected[:channels]) * projected[channels : 2 * channels]
        rights = sigmoid(projected[2 * channels : 3 * channels]) * projected[3 * channels :]
        for half in range(2):
            place = pl.ds((row + half) * pitch, channels)
            lanes = slice(half * tokens, (half + 1) * tokens)
            left_rows[place, :] = lefts[:, lanes]
            right_rows[place, :] = rights[:, lanes]
    for channel in range(channels):
        place = pl.ds(channel, rows, stride=pitch)
        out[channel, 0] = left_rows[place, :].astype(BF16)
        out[channel, 1] = right_rows[place, :].astype(BF16)


def edges(pair, gain, bias, w_left, w_right):
    rows, tokens, channels = pair.shape
    whole = lambda *shape: pl.BlockSpec(shape, lambda step: (0,) * len(shape))
    return pl.pallas_call(
        edges_kernel,
        grid=(rows // ROWS,),
        in_specs=[
            pl.BlockSpec((ROWS, tokens, channels), lambda step: (step, 0, 0)),
            whole(1, channels),
            whole(1, channels),
            whole(channels, 2 * channels),
            whole(channels, 2 * channels),
        ],
        out_specs=pl.BlockSpec((channels, 2, ROWS, tokens), lambda step: (0, 0, step, 0)),
        out_shape=jax.ShapeDtypeStruct((channels, 2, rows, tokens), BF16),
        scratch_shapes=[pltpu.VMEM((4 * channels, channels), BF16)]
        + [pltpu.VMEM((ROWS * (channels + PAD), tokens), F32)] * 2,
        compiler_params=pltpu.CompilerParams(vmem_limit_bytes=16 * 2**20),
        cost_estimate=pl.CostEstimate(
            flops=8 * rows * tokens * channels * channels,
            bytes_accessed=8 * rows * tokens * channels,
            transcendentals=2 * rows * tokens * channels,
        ),
        name="edges",
    )(pair, gain, bias, w_left, w_right)


def gating_kernel(pair, gain, bias, weight, gating):
    rows, tokens, channels = pair.shape
    normed = normalize(pair[...].reshape(rows * tokens, channels), gain[...], bias[...])
    projected = jnp.dot(normed, weight[...], preferred_element_type=F32)
    gating[...] = sigmoid(projected).reshape(rows, tokens, channels)


def gates(pair, gain, bias, weight):
    rows, tokens, channels = pair.shape
    whole = lambda *shape: pl.BlockSpec(shape, lambda step: (0,) * len(shape))
    block = pl.BlockSpec((ROWS, tokens, channels), lambda step: (step, 0, 0))
    return pl.pallas_call(
        gating_kernel,
        grid=(rows // ROWS,),
        in_specs=[block, whole(1, channels), whole(1, channels), whole(channels, channels)],
        out_specs=block,
        out_shape=jax.ShapeDtypeStruct(pair.shape, F32),
        compiler_params=pltpu.CompilerParams(vmem_limit_bytes=16 * 2**20),
        cost_estimate=pl.CostEstimate(
            flops=2 * rows * tokens * channels * channels,
            bytes_accessed=8 * rows * tokens * channels,
            transcendentals=rows * tokens * channels,
        ),
        name="gates",
    )(pair, gain, bias, weight)


def product_kernel(both, out, left_turned, right_whole):
    n_rows, n_cols, _, depth, tokens = both.shape
    for col in range(n_cols):
        lanes = slice(col * tokens, (col + 1) * tokens)
        for row in range(n_rows):
            right_whole[row * depth : (row + 1) * depth, lanes] = both[row, col, 1]
        column = jnp.concatenate([both[row, col, 0] for row in range(n_rows)], axis=0)
        left_turned[lanes, :] = column.T
    wide = 2 * tokens
    for start in range(0, n_cols * tokens, wide):
        total = jnp.dot(
            left_turned[...], right_whole[:, start : start + wide], preferred_element_type=F32
        ).astype(BF16)
        for part in range(2):
            block = total[:, part * tokens : (part + 1) * tokens]
            out[:, start // tokens + part] = block.reshape(n_rows, depth, tokens)


def products(both):
    n_rows, n_cols, _, depth, tokens = both.shape
    size = n_rows * depth
    return pl.pallas_call(
        product_kernel,
        out_shape=jax.ShapeDtypeStruct((n_rows, n_cols, depth, tokens), BF16),
        scratch_shapes=[pltpu.VMEM((size, size), BF16)] * 2,
        compiler_params=pltpu.CompilerParams(vmem_limit_bytes=24 * 2**20),
        cost_estimate=pl.CostEstimate(
            flops=2 * size**3, bytes_accessed=6 * size * size, transcendentals=0
        ),
        name="products",
    )(both)


def update_kernel(product, gating, gain, bias, weight, out, rows_of):
    channels, rows, tokens = product.shape
    values = product[...].astype(F32)
    center = jnp.sum(values, axis=0, keepdims=True) * (1.0 / channels)
    values = values - center
    spread = jnp.sum(values * values, axis=0, keepdims=True) * (1.0 / channels)
    values = values * lax.rsqrt(spread + EPS) * gain[...] + bias[...]
    pitch = rows + PAD
    for channel in range(channels):
        rows_of[pl.ds(channel * pitch, rows), :] = values[channel]
    for row in range(rows):
        normed = rows_of[pl.ds(row, channels, stride=pitch), :].astype(BF16)
        projected = lax.dot_general(
            normed, weight[...], (((0,), (0,)), ((), ())), preferred_element_type=F32
        )
        out[row] = gating[row] * projected


def update(product, gating, gain, bias, weight):
    channels, rows, tokens = product.shape
    whole = lambda *shape: pl.BlockSpec(shape, lambda step: (0,) * len(shape))
    block = pl.BlockSpec((ROWS, tokens, channels), lambda step: (step, 0, 0))
    spread = lambda vector: jnp.broadcast_to(vector[:, None, None], (channels, 1, tokens))
    return pl.pallas_call(
        update_kernel,
        grid=(rows // ROWS,),
        in_specs=[
            pl.BlockSpec((channels, ROWS, tokens), lambda step: (0, step, 0)),
            block,
            whole(channels, 1, tokens),
            whole(channels, 1, tokens),
            whole(channels, channels),
        ],
        out_specs=block,
        out_shape=jax.ShapeDtypeStruct((rows, tokens, channels), F32),
        scratch_shapes=[pltpu.VMEM((channels * (ROWS + PAD), tokens), F32)],
        compiler_params=pltpu.CompilerParams(vmem_limit_bytes=16 * 2**20),
        cost_estimate=pl.CostEstimate(
            flops=2 * rows * tokens * channels * channels,
            bytes_accessed=10 * rows * tokens * channels,
            transcendentals=0,
        ),
        name="update",
    )(product, gating, spread(gain), spread(bias), weight)


def per_device(n_rows, n_cols, pair, ln_gain, ln_bias, w_left, w_right, w_gate, w_out, out_gain, out_bias):
    rows, tokens, channels = pair.shape
    axes = ("row", "col")
    gain, bias = ln_gain[None], ln_bias[None]
    both = edges(pair, gain, bias, w_left, w_right).reshape(channels, 2 * rows, tokens)
    gating = gates(pair, gain, bias, w_gate)
    both = lax.all_to_all(both, axes, 0, 0, tiled=True)
    product = products(both.reshape(n_rows, n_cols, 2, rows, tokens)).reshape(channels, rows, tokens)
    product = lax.all_to_all(product, axes, 0, 0, tiled=True)
    return update(product, gating, out_gain, out_bias, w_out)


def solution(mesh):
    n_rows, n_cols = mesh.shape["row"], mesh.shape["col"]
    return jax.shard_map(
        lambda *args: per_device(n_rows, n_cols, *args),
        mesh=mesh,
        in_specs=(P("row", "col", None), P(), P(), P(), P(), P(), P(), P(), P()),
        out_specs=P("row", "col", None),
        check_vma=False,
    )
```

```python
import jax
import jax.numpy as jnp
from jax import lax
from jax.experimental import pallas as pl
from jax.experimental.pallas import tpu as pltpu
from jax.sharding import PartitionSpec as P

F32, BF16 = jnp.float32, jnp.bfloat16
EPS = 1e-05
ROWS = 16
PAD = 4


def in_hbm(*arrays):
    return [pltpu.with_memory_space_constraint(array, pltpu.HBM) for array in arrays]


def sigmoid(values):
    return 0.5 * jnp.tanh(0.5 * values) + 0.5


def normalize(values, gain, bias):
    center = jnp.mean(values, axis=-1, keepdims=True)
    values = values - center
    spread = jnp.mean(values * values, axis=-1, keepdims=True)
    return (values * lax.rsqrt(spread + EPS) * gain + bias).astype(BF16)


def edges_kernel(
    pair_far, gain_far, bias_far, left_far, right_far, out,
    pair, gain, bias, w_left, w_right, weight, left_rows, right_rows, sems,
):
    rows, tokens, channels = pair.shape
    pitch = channels + PAD
    small = [
        pltpu.make_async_copy(far, near, sems.at[place])
        for place, (far, near) in enumerate(
            [(gain_far, gain), (bias_far, bias), (left_far, w_left), (right_far, w_right)]
        )
    ]

    def fetch(step):
        place = pl.ds(step * ROWS, ROWS)
        return pltpu.make_async_copy(pair_far.at[place], pair.at[place], sems.at[4 + step])

    fetch(0).start()
    for copy in small:
        copy.start()
    for step in range(1, rows // ROWS):
        fetch(step).start()
    for copy in small:
        copy.wait()
    weight[: 2 * channels] = w_left[...].T
    weight[2 * channels :] = w_right[...].T

    def body(step, carry):
        fetch(step).wait()
        base = pl.multiple_of(step * ROWS, ROWS)
        for row in range(0, ROWS, 2):
            values = pair[pl.ds(base + row, 2)].reshape(2 * tokens, channels)
            normed = normalize(values, gain[...], bias[...])
            projected = lax.dot_general(
                weight[...], normed, (((1,), (1,)), ((), ())), preferred_element_type=F32
            )
            lefts = sigmoid(projected[:channels]) * projected[channels : 2 * channels]
            rights = sigmoid(projected[2 * channels : 3 * channels]) * projected[3 * channels :]
            for half in range(2):
                place = pl.ds((row + half) * pitch, channels)
                lanes = slice(half * tokens, (half + 1) * tokens)
                left_rows[place, :] = lefts[:, lanes]
                right_rows[place, :] = rights[:, lanes]
        for channel in range(channels):
            place = pl.ds(channel, ROWS, stride=pitch)
            out[channel, 0, pl.ds(base, ROWS), :] = left_rows[place, :].astype(BF16)
            out[channel, 1, pl.ds(base, ROWS), :] = right_rows[place, :].astype(BF16)
        return carry

    lax.fori_loop(0, rows // ROWS, body, 0)


def edges(pair, gain, bias, w_left, w_right):
    rows, tokens, channels = pair.shape
    far = pl.BlockSpec(memory_space=pltpu.HBM)
    return pl.pallas_call(
        edges_kernel,
        in_specs=[far] * 5,
        out_specs=pl.BlockSpec(memory_space=pltpu.VMEM),
        out_shape=jax.ShapeDtypeStruct((channels, 2, rows, tokens), BF16),
        scratch_shapes=[
            pltpu.VMEM(pair.shape, F32),
            pltpu.VMEM(gain.shape, F32),
            pltpu.VMEM(bias.shape, F32),
            pltpu.VMEM(w_left.shape, BF16),
            pltpu.VMEM(w_right.shape, BF16),
            pltpu.VMEM((4 * channels, channels), BF16),
            pltpu.VMEM((ROWS * (channels + PAD), tokens), F32),
            pltpu.VMEM((ROWS * (channels + PAD), tokens), F32),
            pltpu.SemaphoreType.DMA((4 + rows // ROWS,)),
        ],
        compiler_params=pltpu.CompilerParams(vmem_limit_bytes=20 * 2**20),
        cost_estimate=pl.CostEstimate(
            flops=8 * rows * tokens * channels * channels,
            bytes_accessed=8 * rows * tokens * channels,
            transcendentals=2 * rows * tokens * channels,
        ),
        name="edges",
    )(*in_hbm(pair, gain, bias, w_left, w_right))


def gating_kernel(pair, gain, bias, weight, gating):
    rows, tokens, channels = pair.shape
    normed = normalize(pair[...].reshape(rows * tokens, channels), gain[...], bias[...])
    projected = jnp.dot(normed, weight[...], preferred_element_type=F32)
    gating[...] = sigmoid(projected).reshape(rows, tokens, channels)


def gates(pair, gain, bias, weight):
    rows, tokens, channels = pair.shape
    whole = lambda *shape: pl.BlockSpec(shape, lambda step: (0,) * len(shape))
    block = pl.BlockSpec((ROWS, tokens, channels), lambda step: (step, 0, 0))
    return pl.pallas_call(
        gating_kernel,
        grid=(rows // ROWS,),
        in_specs=[block, whole(1, channels), whole(1, channels), whole(channels, channels)],
        out_specs=block,
        out_shape=jax.ShapeDtypeStruct(pair.shape, F32),
        compiler_params=pltpu.CompilerParams(vmem_limit_bytes=16 * 2**20),
        cost_estimate=pl.CostEstimate(
            flops=2 * rows * tokens * channels * channels,
            bytes_accessed=8 * rows * tokens * channels,
            transcendentals=rows * tokens * channels,
        ),
        name="gates",
    )(pair, gain, bias, weight)


def product_kernel(both, out_far, left_turned, right_whole, out, sems):
    n_rows, n_cols, _, depth, tokens = both.shape
    for col in range(n_cols):
        lanes = slice(col * tokens, (col + 1) * tokens)
        for row in range(n_rows):
            right_whole[row * depth : (row + 1) * depth, lanes] = both[row, col, 1]
        column = jnp.concatenate([both[row, col, 0] for row in range(n_rows)], axis=0)
        left_turned[lanes, :] = column.T
    copies = []
    for col in range(0, n_cols, 2):
        total = jnp.dot(
            left_turned[...],
            right_whole[:, col * tokens : (col + 2) * tokens],
            preferred_element_type=F32,
        ).astype(BF16)
        for part in range(2):
            block = total[:, part * tokens : (part + 1) * tokens]
            out[:, col + part] = block.reshape(n_rows, depth, tokens)
        place = pl.ds(col, 2)
        copies.append(
            pltpu.make_async_copy(out.at[:, place], out_far.at[:, place], sems.at[col // 2])
        )
        copies[-1].start()
    for copy in copies:
        copy.wait()


def products(both):
    n_rows, n_cols, _, depth, tokens = both.shape
    size = n_rows * depth
    shape = (n_rows, n_cols, depth, tokens)
    return pl.pallas_call(
        product_kernel,
        in_specs=[pl.BlockSpec(memory_space=pltpu.VMEM)],
        out_specs=pl.BlockSpec(memory_space=pltpu.HBM),
        out_shape=jax.ShapeDtypeStruct(shape, BF16),
        scratch_shapes=[pltpu.VMEM((size, size), BF16)] * 2
        + [pltpu.VMEM(shape, BF16), pltpu.SemaphoreType.DMA((n_cols // 2,))],
        compiler_params=pltpu.CompilerParams(vmem_limit_bytes=24 * 2**20),
        cost_estimate=pl.CostEstimate(
            flops=2 * size**3, bytes_accessed=6 * size * size, transcendentals=0
        ),
        name="products",
    )(both)


def update_kernel(
    product, gating_far, gain_far, bias_far, weight_far, out_far,
    gating, gain, bias, weight, gains, biases, rows_of, out, sems,
):
    channels, rows, tokens = product.shape
    pitch = ROWS + PAD
    steps = rows // ROWS
    small = [
        pltpu.make_async_copy(far, near, sems.at[place])
        for place, (far, near) in enumerate(
            [(gain_far, gain), (bias_far, bias), (weight_far, weight)]
        )
    ]

    def fetch(step):
        place = pl.ds(step * ROWS, ROWS)
        return pltpu.make_async_copy(gating_far.at[place], gating.at[place], sems.at[3 + step])

    def send(step):
        place = pl.ds(step * ROWS, ROWS)
        return pltpu.make_async_copy(out.at[place], out_far.at[place], sems.at[3 + steps + step])

    for copy in small:
        copy.start()
    for step in range(steps):
        fetch(step).start()
    for copy in small:
        copy.wait()
    gains[...] = jnp.broadcast_to(gain[...], (tokens, channels)).T
    biases[...] = jnp.broadcast_to(bias[...], (tokens, channels)).T

    def body(step, carry):
        base = pl.multiple_of(step * ROWS, ROWS)
        load = lambda channel: product[channel, pl.ds(base, ROWS), :].astype(F32)
        center = load(0)
        for channel in range(1, channels):
            center = center + load(channel)
        center = center * (1.0 / channels)
        spread = jnp.zeros_like(center)
        for channel in range(channels):
            offset = load(channel) - center
            spread = spread + offset * offset
        scale = lax.rsqrt(spread * (1.0 / channels) + EPS)
        for channel in range(channels):
            normed = (load(channel) - center) * scale
            normed = normed * gains[channel : channel + 1, :] + biases[channel : channel + 1, :]
            rows_of[pl.ds(channel * pitch, ROWS), :] = normed
        fetch(step).wait()
        for row in range(ROWS):
            normed = rows_of[pl.ds(row, channels, stride=pitch), :].astype(BF16)
            projected = lax.dot_general(
                normed, weight[...], (((0,), (0,)), ((), ())), preferred_element_type=F32
            )
            out[base + row] = gating[base + row] * projected
        send(step).start()
        return carry

    lax.fori_loop(0, steps, body, 0)
    for step in range(steps):
        send(step).wait()


def update(product, gating, gain, bias, weight):
    channels, rows, tokens = product.shape
    far = pl.BlockSpec(memory_space=pltpu.HBM)
    return pl.pallas_call(
        update_kernel,
        in_specs=[pl.BlockSpec(memory_space=pltpu.VMEM), far, far, far, far],
        out_specs=far,
        out_shape=jax.ShapeDtypeStruct((rows, tokens, channels), F32),
        scratch_shapes=[
            pltpu.VMEM(gating.shape, F32),
            pltpu.VMEM(gain.shape, F32),
            pltpu.VMEM(bias.shape, F32),
            pltpu.VMEM(weight.shape, BF16),
            pltpu.VMEM((channels, tokens), F32),
            pltpu.VMEM((channels, tokens), F32),
            pltpu.VMEM((channels * (ROWS + PAD), tokens), F32),
            pltpu.VMEM((rows, tokens, channels), F32),
            pltpu.SemaphoreType.DMA((3 + 2 * (rows // ROWS),)),
        ],
        compiler_params=pltpu.CompilerParams(vmem_limit_bytes=20 * 2**20),
        cost_estimate=pl.CostEstimate(
            flops=2 * rows * tokens * channels * channels,
            bytes_accessed=10 * rows * tokens * channels,
            transcendentals=0,
        ),
        name="update",
    )(product, *in_hbm(gating, gain, bias, weight))


def per_device(n_rows, n_cols, pair, ln_gain, ln_bias, w_left, w_right, w_gate, w_out, out_gain, out_bias):
    rows, tokens, channels = pair.shape
    axes = ("row", "col")
    gain, bias = ln_gain[None], ln_bias[None]
    both = edges(pair, gain, bias, w_left, w_right).reshape(channels, 2 * rows, tokens)
    gating = gates(pair, gain, bias, w_gate)
    both = lax.all_to_all(both, axes, 0, 0, tiled=True)
    product = products(both.reshape(n_rows, n_cols, 2, rows, tokens)).reshape(channels, rows, tokens)
    product = lax.all_to_all(product, axes, 0, 0, tiled=True)
    return update(product, gating, out_gain[None], out_bias[None], w_out)


def solution(mesh):
    n_rows, n_cols = mesh.shape["row"], mesh.shape["col"]
    return jax.shard_map(
        lambda *args: per_device(n_rows, n_cols, *args),
        mesh=mesh,
        in_specs=(P("row", "col", None), P(), P(), P(), P(), P(), P(), P(), P()),
        out_specs=P("row", "col", None),
        check_vma=False,
    )
```

```python
import jax
import jax.numpy as jnp
from jax import lax
from jax.experimental import pallas as pl
from jax.experimental.pallas import tpu as pltpu
from jax.sharding import PartitionSpec as P

F32, BF16 = jnp.float32, jnp.bfloat16
EPS = 1e-05
ROWS = 16
PAD = 4


def in_hbm(*arrays):
    return [pltpu.with_memory_space_constraint(array, pltpu.HBM) for array in arrays]


def sigmoid(values):
    return 0.5 * jnp.tanh(0.5 * values) + 0.5


def normalize(values, gain, bias):
    center = jnp.mean(values, axis=-1, keepdims=True)
    values = values - center
    spread = jnp.mean(values * values, axis=-1, keepdims=True)
    return (values * lax.rsqrt(spread + EPS) * gain + bias).astype(BF16)


def edges_kernel(
    pair_far, gain_far, bias_far, left_far, right_far, out,
    pair, gain, bias, w_left, w_right, weight, left_rows, right_rows, sems,
):
    rows, tokens, channels = pair.shape
    pitch = channels + PAD
    small = [
        pltpu.make_async_copy(far, near, sems.at[place])
        for place, (far, near) in enumerate(
            [(gain_far, gain), (bias_far, bias), (left_far, w_left), (right_far, w_right)]
        )
    ]

    def fetch(step):
        place = pl.ds(step * ROWS, ROWS)
        return pltpu.make_async_copy(pair_far.at[place], pair.at[place], sems.at[4 + step])

    fetch(0).start()
    for copy in small:
        copy.start()
    for step in range(1, rows // ROWS):
        fetch(step).start()
    for copy in small:
        copy.wait()
    weight[: 2 * channels] = w_left[...].T
    weight[2 * channels :] = w_right[...].T

    gains = jnp.broadcast_to(gain[...], (2 * tokens, channels)).T
    biases = jnp.broadcast_to(bias[...], (2 * tokens, channels)).T

    def body(step, carry):
        fetch(step).wait()
        base = pl.multiple_of(step * ROWS, ROWS)
        for row in range(0, ROWS, 2):
            values = pair[pl.ds(base + row, 2)].reshape(2 * tokens, channels).T
            center = jnp.sum(values, axis=0, keepdims=True) * (1.0 / channels)
            values = values - center
            spread = jnp.sum(values * values, axis=0, keepdims=True) * (1.0 / channels)
            normed = values * lax.rsqrt(spread + EPS) * gains + biases
            projected = jnp.dot(weight[...], normed.astype(BF16), preferred_element_type=F32)
            lefts = sigmoid(projected[:channels]) * projected[channels : 2 * channels]
            rights = sigmoid(projected[2 * channels : 3 * channels]) * projected[3 * channels :]
            for half in range(2):
                place = pl.ds((row + half) * pitch, channels)
                lanes = slice(half * tokens, (half + 1) * tokens)
                left_rows[place, :] = lefts[:, lanes]
                right_rows[place, :] = rights[:, lanes]
        for channel in range(channels):
            place = pl.ds(channel, ROWS, stride=pitch)
            out[channel, 0, pl.ds(base, ROWS), :] = left_rows[place, :].astype(BF16)
            out[channel, 1, pl.ds(base, ROWS), :] = right_rows[place, :].astype(BF16)
        return carry

    lax.fori_loop(0, rows // ROWS, body, 0)


def edges(pair, gain, bias, w_left, w_right):
    rows, tokens, channels = pair.shape
    far = pl.BlockSpec(memory_space=pltpu.HBM)
    return pl.pallas_call(
        edges_kernel,
        in_specs=[far] * 5,
        out_specs=pl.BlockSpec(memory_space=pltpu.VMEM),
        out_shape=jax.ShapeDtypeStruct((channels, 2, rows, tokens), BF16),
        scratch_shapes=[
            pltpu.VMEM(pair.shape, F32),
            pltpu.VMEM(gain.shape, F32),
            pltpu.VMEM(bias.shape, F32),
            pltpu.VMEM(w_left.shape, BF16),
            pltpu.VMEM(w_right.shape, BF16),
            pltpu.VMEM((4 * channels, channels), BF16),
            pltpu.VMEM((ROWS * (channels + PAD), tokens), F32),
            pltpu.VMEM((ROWS * (channels + PAD), tokens), F32),
            pltpu.SemaphoreType.DMA((4 + rows // ROWS,)),
        ],
        compiler_params=pltpu.CompilerParams(vmem_limit_bytes=20 * 2**20),
        cost_estimate=pl.CostEstimate(
            flops=8 * rows * tokens * channels * channels,
            bytes_accessed=8 * rows * tokens * channels,
            transcendentals=2 * rows * tokens * channels,
        ),
        name="edges",
    )(*in_hbm(pair, gain, bias, w_left, w_right))


def gating_kernel(pair, gain, bias, weight, gating):
    rows, tokens, channels = pair.shape
    normed = normalize(pair[...].reshape(rows * tokens, channels), gain[...], bias[...])
    projected = jnp.dot(normed, weight[...], preferred_element_type=F32)
    gating[...] = sigmoid(projected).reshape(rows, tokens, channels)


def gates(pair, gain, bias, weight):
    rows, tokens, channels = pair.shape
    whole = lambda *shape: pl.BlockSpec(shape, lambda step: (0,) * len(shape))
    block = pl.BlockSpec((ROWS, tokens, channels), lambda step: (step, 0, 0))
    return pl.pallas_call(
        gating_kernel,
        grid=(rows // ROWS,),
        in_specs=[block, whole(1, channels), whole(1, channels), whole(channels, channels)],
        out_specs=block,
        out_shape=jax.ShapeDtypeStruct(pair.shape, F32),
        compiler_params=pltpu.CompilerParams(vmem_limit_bytes=16 * 2**20),
        cost_estimate=pl.CostEstimate(
            flops=2 * rows * tokens * channels * channels,
            bytes_accessed=8 * rows * tokens * channels,
            transcendentals=rows * tokens * channels,
        ),
        name="gates",
    )(pair, gain, bias, weight)


def product_kernel(both, out_far, left_turned, right_whole, out, sems):
    n_rows, n_cols, _, depth, tokens = both.shape
    for col in range(n_cols):
        lanes = slice(col * tokens, (col + 1) * tokens)
        for row in range(n_rows):
            right_whole[row * depth : (row + 1) * depth, lanes] = both[row, col, 1]
        column = jnp.concatenate([both[row, col, 0] for row in range(n_rows)], axis=0)
        left_turned[lanes, :] = column.T
    copies = []
    for col in range(0, n_cols, 2):
        total = jnp.dot(
            left_turned[...],
            right_whole[:, col * tokens : (col + 2) * tokens],
            preferred_element_type=F32,
        ).astype(BF16)
        for part in range(2):
            block = total[:, part * tokens : (part + 1) * tokens]
            out[:, col + part] = block.reshape(n_rows, depth, tokens)
        place = pl.ds(col, 2)
        copies.append(
            pltpu.make_async_copy(out.at[:, place], out_far.at[:, place], sems.at[col // 2])
        )
        copies[-1].start()
    for copy in copies:
        copy.wait()


def products(both):
    n_rows, n_cols, _, depth, tokens = both.shape
    size = n_rows * depth
    shape = (n_rows, n_cols, depth, tokens)
    return pl.pallas_call(
        product_kernel,
        in_specs=[pl.BlockSpec(memory_space=pltpu.VMEM)],
        out_specs=pl.BlockSpec(memory_space=pltpu.HBM),
        out_shape=pltpu.HBM(shape, BF16),
        scratch_shapes=[pltpu.VMEM((size, size), BF16)] * 2
        + [pltpu.VMEM(shape, BF16), pltpu.SemaphoreType.DMA((n_cols // 2,))],
        compiler_params=pltpu.CompilerParams(vmem_limit_bytes=24 * 2**20),
        cost_estimate=pl.CostEstimate(
            flops=2 * size**3, bytes_accessed=6 * size * size, transcendentals=0
        ),
        name="products",
    )(both)


def update_kernel(
    product, gating_far, gain, bias, weight, out_far, gating, gains, biases, rows_of, out, sems
):
    channels, rows, tokens = product.shape
    pitch = ROWS + PAD
    steps = rows // ROWS
    def fetch(step):
        place = pl.ds(step * ROWS, ROWS)
        return pltpu.make_async_copy(gating_far.at[place], gating.at[place], sems.at[step])

    def send(step):
        place = pl.ds(step * ROWS, ROWS)
        return pltpu.make_async_copy(out.at[place], out_far.at[place], sems.at[steps + step])

    for step in range(steps):
        fetch(step).start()
    gains[...] = jnp.broadcast_to(gain[...], (tokens, channels)).T
    biases[...] = jnp.broadcast_to(bias[...], (tokens, channels)).T

    def body(step, carry):
        base = pl.multiple_of(step * ROWS, ROWS)
        load = lambda channel: product[channel, pl.ds(base, ROWS), :].astype(F32)
        center = load(0)
        for channel in range(1, channels):
            center = center + load(channel)
        center = center * (1.0 / channels)
        spread = jnp.zeros_like(center)
        for channel in range(channels):
            offset = load(channel) - center
            spread = spread + offset * offset
        scale = lax.rsqrt(spread * (1.0 / channels) + EPS)
        for channel in range(channels):
            normed = (load(channel) - center) * scale
            normed = normed * gains[channel : channel + 1, :] + biases[channel : channel + 1, :]
            rows_of[pl.ds(channel * pitch, ROWS), :] = normed
        fetch(step).wait()
        for row in range(ROWS):
            normed = rows_of[pl.ds(row, channels, stride=pitch), :].astype(BF16)
            projected = lax.dot_general(
                normed, weight[...], (((0,), (0,)), ((), ())), preferred_element_type=F32
            )
            out[base + row] = gating[base + row] * projected
        send(step).start()
        return carry

    lax.fori_loop(0, steps, body, 0)
    for step in range(steps):
        send(step).wait()


def update(product, gating, gain, bias, weight):
    channels, rows, tokens = product.shape
    near, far = pl.BlockSpec(memory_space=pltpu.VMEM), pl.BlockSpec(memory_space=pltpu.HBM)
    return pl.pallas_call(
        update_kernel,
        in_specs=[near, far, near, near, near],
        out_specs=far,
        out_shape=jax.ShapeDtypeStruct((rows, tokens, channels), F32),
        scratch_shapes=[
            pltpu.VMEM(gating.shape, F32),
            pltpu.VMEM((channels, tokens), F32),
            pltpu.VMEM((channels, tokens), F32),
            pltpu.VMEM((channels * (ROWS + PAD), tokens), F32),
            pltpu.VMEM((rows, tokens, channels), F32),
            pltpu.SemaphoreType.DMA((2 * (rows // ROWS),)),
        ],
        compiler_params=pltpu.CompilerParams(vmem_limit_bytes=20 * 2**20),
        cost_estimate=pl.CostEstimate(
            flops=2 * rows * tokens * channels * channels,
            bytes_accessed=10 * rows * tokens * channels,
            transcendentals=0,
        ),
        name="update",
    )(product, *in_hbm(gating), gain, bias, weight)


def per_device(n_rows, n_cols, pair, ln_gain, ln_bias, w_left, w_right, w_gate, w_out, out_gain, out_bias):
    rows, tokens, channels = pair.shape
    axes = ("row", "col")
    gain, bias = ln_gain[None], ln_bias[None]
    both = edges(pair, gain, bias, w_left, w_right).reshape(channels, 2 * rows, tokens)
    gating = gates(pair, gain, bias, w_gate)
    both = lax.all_to_all(both, axes, 0, 0, tiled=True)
    product = products(both.reshape(n_rows, n_cols, 2, rows, tokens)).reshape(channels, rows, tokens)
    product = lax.all_to_all(product, axes, 0, 0, tiled=True)
    return update(product, gating, out_gain[None], out_bias[None], w_out)


def solution(mesh):
    n_rows, n_cols = mesh.shape["row"], mesh.shape["col"]
    return jax.shard_map(
        lambda *args: per_device(n_rows, n_cols, *args),
        mesh=mesh,
        in_specs=(P("row", "col", None), P(), P(), P(), P(), P(), P(), P(), P()),
        out_specs=P("row", "col", None),
        check_vma=False,
    )
```

```python
import jax
import jax.numpy as jnp
from jax import lax
from jax.experimental import pallas as pl
from jax.experimental.pallas import tpu as pltpu
from jax.sharding import PartitionSpec as P

F32, BF16 = jnp.float32, jnp.bfloat16
EPS = 1e-05
ROWS = 16
PAD = 4


def in_hbm(*arrays):
    return [pltpu.with_memory_space_constraint(array, pltpu.HBM) for array in arrays]


def sigmoid(values):
    return 0.5 * jnp.tanh(0.5 * values) + 0.5


def edges_kernel(
    pair_far, gain_far, bias_far, left_far, right_far, gate_far, out, gating,
    pair, gain, bias, w_left, w_right, w_gate, weight, left_rows, right_rows, sems,
):
    rows, tokens, channels = pair.shape
    pitch = channels + PAD
    small = [
        pltpu.make_async_copy(far, near, sems.at[place])
        for place, (far, near) in enumerate(
            zip(
                (gain_far, bias_far, left_far, right_far, gate_far),
                (gain, bias, w_left, w_right, w_gate),
            )
        )
    ]

    def fetch(step):
        place = pl.ds(step * ROWS, ROWS)
        return pltpu.make_async_copy(pair_far.at[place], pair.at[place], sems.at[5 + step])

    fetch(0).start()
    for copy in small:
        copy.start()
    for step in range(1, rows // ROWS):
        fetch(step).start()
    for copy in small:
        copy.wait()
    weight[: 2 * channels] = w_left[...].T
    weight[2 * channels :] = w_right[...].T

    gains = jnp.broadcast_to(gain[...], (2 * tokens, channels)).T
    biases = jnp.broadcast_to(bias[...], (2 * tokens, channels)).T

    def body(step, carry):
        fetch(step).wait()
        base = pl.multiple_of(step * ROWS, ROWS)
        for row in range(0, ROWS, 2):
            values = pair[pl.ds(base + row, 2)].reshape(2 * tokens, channels).T
            center = jnp.sum(values, axis=0, keepdims=True) * (1.0 / channels)
            values = values - center
            spread = jnp.sum(values * values, axis=0, keepdims=True) * (1.0 / channels)
            normed = (values * lax.rsqrt(spread + EPS) * gains + biases).astype(BF16)
            projected = jnp.dot(weight[...], normed, preferred_element_type=F32)
            gates = lax.dot_general(
                normed, w_gate[...], (((0,), (0,)), ((), ())), preferred_element_type=F32
            )
            gating[pl.ds(base + row, 2)] = sigmoid(gates).reshape(2, tokens, channels)
            lefts = sigmoid(projected[:channels]) * projected[channels : 2 * channels]
            rights = sigmoid(projected[2 * channels : 3 * channels]) * projected[3 * channels :]
            for half in range(2):
                place = pl.ds((row + half) * pitch, channels)
                lanes = slice(half * tokens, (half + 1) * tokens)
                left_rows[place, :] = lefts[:, lanes]
                right_rows[place, :] = rights[:, lanes]
        for channel in range(channels):
            place = pl.ds(channel, ROWS, stride=pitch)
            out[channel, 0, pl.ds(base, ROWS), :] = left_rows[place, :].astype(BF16)
            out[channel, 1, pl.ds(base, ROWS), :] = right_rows[place, :].astype(BF16)
        return carry

    lax.fori_loop(0, rows // ROWS, body, 0)


def edges(pair, gain, bias, w_left, w_right, w_gate):
    rows, tokens, channels = pair.shape
    far = pl.BlockSpec(memory_space=pltpu.HBM)
    return pl.pallas_call(
        edges_kernel,
        in_specs=[far] * 6,
        out_specs=[pl.BlockSpec(memory_space=pltpu.VMEM)] * 2,
        out_shape=[
            jax.ShapeDtypeStruct((channels, 2, rows, tokens), BF16),
            jax.ShapeDtypeStruct(pair.shape, F32),
        ],
        scratch_shapes=[
            pltpu.VMEM(pair.shape, F32),
            pltpu.VMEM(gain.shape, F32),
            pltpu.VMEM(bias.shape, F32),
            pltpu.VMEM(w_left.shape, BF16),
            pltpu.VMEM(w_right.shape, BF16),
            pltpu.VMEM(w_gate.shape, BF16),
            pltpu.VMEM((4 * channels, channels), BF16),
            pltpu.VMEM((ROWS * (channels + PAD), tokens), F32),
            pltpu.VMEM((ROWS * (channels + PAD), tokens), F32),
            pltpu.SemaphoreType.DMA((5 + rows // ROWS,)),
        ],
        compiler_params=pltpu.CompilerParams(vmem_limit_bytes=20 * 2**20),
        cost_estimate=pl.CostEstimate(
            flops=10 * rows * tokens * channels * channels,
            bytes_accessed=12 * rows * tokens * channels,
            transcendentals=3 * rows * tokens * channels,
        ),
        name="edges",
    )(*in_hbm(pair, gain, bias, w_left, w_right, w_gate))


def product_kernel(both, out, left_turned, right_whole):
    n_rows, n_cols, _, depth, tokens = both.shape
    for col in range(n_cols):
        lanes = slice(col * tokens, (col + 1) * tokens)
        for row in range(n_rows):
            right_whole[row * depth : (row + 1) * depth, lanes] = both[row, col, 1]
        column = jnp.concatenate([both[row, col, 0] for row in range(n_rows)], axis=0)
        left_turned[lanes, :] = column.T
    for col in range(0, n_cols, 2):
        total = jnp.dot(
            left_turned[...],
            right_whole[:, col * tokens : (col + 2) * tokens],
            preferred_element_type=F32,
        ).astype(BF16)
        for part in range(2):
            block = total[:, part * tokens : (part + 1) * tokens]
            out[:, col + part] = block.reshape(n_rows, depth, tokens)


def products(both):
    n_rows, n_cols, _, depth, tokens = both.shape
    size = n_rows * depth
    return pl.pallas_call(
        product_kernel,
        out_shape=jax.ShapeDtypeStruct((n_rows, n_cols, depth, tokens), BF16),
        scratch_shapes=[pltpu.VMEM((size, size), BF16)] * 2,
        compiler_params=pltpu.CompilerParams(vmem_limit_bytes=24 * 2**20),
        cost_estimate=pl.CostEstimate(
            flops=2 * size**3, bytes_accessed=6 * size * size, transcendentals=0
        ),
        name="products",
    )(both)


def update_kernel(
    product, gating, gain, bias, weight, out_far, gains, biases, rows_of, out, sems
):
    channels, rows, tokens = product.shape
    pitch = ROWS + PAD
    steps = rows // ROWS
    def send(step):
        place = pl.ds(step * ROWS, ROWS)
        return pltpu.make_async_copy(out.at[place], out_far.at[place], sems.at[step])

    gains[...] = jnp.broadcast_to(gain[...], (tokens, channels)).T
    biases[...] = jnp.broadcast_to(bias[...], (tokens, channels)).T

    def body(step, carry):
        base = pl.multiple_of(step * ROWS, ROWS)
        load = lambda channel: product[channel, pl.ds(base, ROWS), :].astype(F32)
        center = load(0)
        for channel in range(1, channels):
            center = center + load(channel)
        center = center * (1.0 / channels)
        spread = jnp.zeros_like(center)
        for channel in range(channels):
            offset = load(channel) - center
            spread = spread + offset * offset
        scale = lax.rsqrt(spread * (1.0 / channels) + EPS)
        for channel in range(channels):
            normed = (load(channel) - center) * scale
            normed = normed * gains[channel : channel + 1, :] + biases[channel : channel + 1, :]
            rows_of[pl.ds(channel * pitch, ROWS), :] = normed
        for row in range(ROWS):
            normed = rows_of[pl.ds(row, channels, stride=pitch), :].astype(BF16)
            projected = lax.dot_general(
                normed, weight[...], (((0,), (0,)), ((), ())), preferred_element_type=F32
            )
            out[base + row] = gating[base + row] * projected
        send(step).start()
        return carry

    lax.fori_loop(0, steps, body, 0)
    for step in range(steps):
        send(step).wait()


def update(product, gating, gain, bias, weight):
    channels, rows, tokens = product.shape
    return pl.pallas_call(
        update_kernel,
        in_specs=[pl.BlockSpec(memory_space=pltpu.VMEM)] * 5,
        out_specs=pl.BlockSpec(memory_space=pltpu.HBM),
        out_shape=jax.ShapeDtypeStruct((rows, tokens, channels), F32),
        scratch_shapes=[
            pltpu.VMEM((channels, tokens), F32),
            pltpu.VMEM((channels, tokens), F32),
            pltpu.VMEM((channels * (ROWS + PAD), tokens), F32),
            pltpu.VMEM((rows, tokens, channels), F32),
            pltpu.SemaphoreType.DMA((rows // ROWS,)),
        ],
        compiler_params=pltpu.CompilerParams(vmem_limit_bytes=20 * 2**20),
        cost_estimate=pl.CostEstimate(
            flops=2 * rows * tokens * channels * channels,
            bytes_accessed=10 * rows * tokens * channels,
            transcendentals=0,
        ),
        name="update",
    )(product, gating, gain, bias, weight)


def per_device(n_rows, n_cols, pair, ln_gain, ln_bias, w_left, w_right, w_gate, w_out, out_gain, out_bias):
    rows, tokens, channels = pair.shape
    axes = ("row", "col")
    gain, bias = ln_gain[None], ln_bias[None]
    both, gating = edges(pair, gain, bias, w_left, w_right, w_gate)
    both = lax.all_to_all(both.reshape(channels, 2 * rows, tokens), axes, 0, 0, tiled=True)
    product = products(both.reshape(n_rows, n_cols, 2, rows, tokens)).reshape(channels, rows, tokens)
    product = lax.all_to_all(product, axes, 0, 0, tiled=True)
    return update(product, gating, out_gain[None], out_bias[None], w_out)


def solution(mesh):
    n_rows, n_cols = mesh.shape["row"], mesh.shape["col"]
    return jax.shard_map(
        lambda *args: per_device(n_rows, n_cols, *args),
        mesh=mesh,
        in_specs=(P("row", "col", None), P(), P(), P(), P(), P(), P(), P(), P()),
        out_specs=P("row", "col", None),
        check_vma=False,
    )
```

```python
import jax
import jax.numpy as jnp
from jax import lax
from jax.experimental import pallas as pl
from jax.experimental.pallas import tpu as pltpu
from jax.sharding import PartitionSpec as P

F32, BF16 = jnp.float32, jnp.bfloat16
EPS = 1e-05
ROWS = 16
BATCH = 4
SEND = 4
PAD = 4


def in_hbm(*arrays):
    return [pltpu.with_memory_space_constraint(array, pltpu.HBM) for array in arrays]


def edges_kernel(
    pair_far, gain_far, bias_far, left_far, right_far, gate_far, out, gating,
    pair, gain, bias, w_left, w_right, w_gate, weight, left_rows, right_rows, sems,
):
    rows, tokens, channels = pair.shape
    pitch = channels + PAD
    small = [
        pltpu.make_async_copy(far, near, sems.at[place])
        for place, (far, near) in enumerate(
            zip(
                (gain_far, bias_far, left_far, right_far, gate_far),
                (gain, bias, w_left, w_right, w_gate),
            )
        )
    ]

    def fetch(step):
        place = pl.ds(step * ROWS, ROWS)
        return pltpu.make_async_copy(pair_far.at[place], pair.at[place], sems.at[5 + step])

    fetch(0).start()
    for copy in small:
        copy.start()
    for step in range(1, rows // ROWS):
        fetch(step).start()
    for copy in small:
        copy.wait()
    weight[: 2 * channels] = w_left[...].T * 0.5
    weight[2 * channels :] = w_right[...].T * 0.5
    w_gate[...] = w_gate[...] * 0.5

    gains = jnp.broadcast_to(gain[...], (BATCH * tokens, channels)).T
    biases = jnp.broadcast_to(bias[...], (BATCH * tokens, channels)).T

    def body(step, carry):
        fetch(step).wait()
        base = pl.multiple_of(step * ROWS, ROWS)
        for row in range(0, ROWS, BATCH):
            values = pair[pl.ds(base + row, BATCH)].reshape(BATCH * tokens, channels).T
            center = jnp.sum(values, axis=0, keepdims=True) * (1.0 / channels)
            values = values - center
            spread = jnp.sum(values * values, axis=0, keepdims=True) * (1.0 / channels)
            normed = (values * lax.rsqrt(spread + EPS) * gains + biases).astype(BF16)
            projected = jnp.dot(weight[...], normed, preferred_element_type=F32)
            gates = lax.dot_general(
                normed, w_gate[...], (((0,), (0,)), ((), ())), preferred_element_type=F32
            )
            gating[pl.ds(base + row, BATCH)] = 0.5 * jnp.tanh(gates).reshape(BATCH, tokens, channels) + 0.5
            gate_left, left, gate_right, right = jnp.split(projected, 4, axis=0)
            lefts = (jnp.tanh(gate_left) + 1.0) * left
            rights = (jnp.tanh(gate_right) + 1.0) * right
            for part in range(BATCH):
                place = pl.ds((row + part) * pitch, channels)
                lanes = slice(part * tokens, (part + 1) * tokens)
                left_rows[place, :] = lefts[:, lanes]
                right_rows[place, :] = rights[:, lanes]
        for channel in range(channels):
            place = pl.ds(channel, ROWS, stride=pitch)
            out[channel, 0, pl.ds(base, ROWS), :] = left_rows[place, :].astype(BF16)
            out[channel, 1, pl.ds(base, ROWS), :] = right_rows[place, :].astype(BF16)
        return carry

    lax.fori_loop(0, rows // ROWS, body, 0)


def edges(pair, gain, bias, w_left, w_right, w_gate):
    rows, tokens, channels = pair.shape
    far = pl.BlockSpec(memory_space=pltpu.HBM)
    return pl.pallas_call(
        edges_kernel,
        in_specs=[far] * 6,
        out_specs=[pl.BlockSpec(memory_space=pltpu.VMEM)] * 2,
        out_shape=[
            jax.ShapeDtypeStruct((channels, 2, rows, tokens), BF16),
            jax.ShapeDtypeStruct(pair.shape, F32),
        ],
        scratch_shapes=[
            pltpu.VMEM(pair.shape, F32),
            pltpu.VMEM(gain.shape, F32),
            pltpu.VMEM(bias.shape, F32),
            pltpu.VMEM(w_left.shape, BF16),
            pltpu.VMEM(w_right.shape, BF16),
            pltpu.VMEM(w_gate.shape, BF16),
            pltpu.VMEM((4 * channels, channels), BF16),
            pltpu.VMEM((ROWS * (channels + PAD), tokens), F32),
            pltpu.VMEM((ROWS * (channels + PAD), tokens), F32),
            pltpu.SemaphoreType.DMA((5 + rows // ROWS,)),
        ],
        compiler_params=pltpu.CompilerParams(vmem_limit_bytes=20 * 2**20),
        cost_estimate=pl.CostEstimate(
            flops=10 * rows * tokens * channels * channels,
            bytes_accessed=12 * rows * tokens * channels,
            transcendentals=3 * rows * tokens * channels,
        ),
        name="edges",
    )(*in_hbm(pair, gain, bias, w_left, w_right, w_gate))


def product_kernel(both, out, left_turned, right_whole):
    n_rows, n_cols, _, depth, tokens = both.shape
    for col in range(n_cols):
        lanes = slice(col * tokens, (col + 1) * tokens)
        for row in range(n_rows):
            right_whole[row * depth : (row + 1) * depth, lanes] = both[row, col, 1]
        column = jnp.concatenate([both[row, col, 0] for row in range(n_rows)], axis=0)
        left_turned[lanes, :] = column.T
    for col in range(0, n_cols, 2):
        total = jnp.dot(
            left_turned[...],
            right_whole[:, col * tokens : (col + 2) * tokens],
            preferred_element_type=F32,
        ).astype(BF16)
        for part in range(2):
            block = total[:, part * tokens : (part + 1) * tokens]
            out[:, col + part] = block.reshape(n_rows, depth, tokens)


def products(both):
    n_rows, n_cols, _, depth, tokens = both.shape
    size = n_rows * depth
    return pl.pallas_call(
        product_kernel,
        out_shape=jax.ShapeDtypeStruct((n_rows, n_cols, depth, tokens), BF16),
        scratch_shapes=[pltpu.VMEM((size, size), BF16)] * 2,
        compiler_params=pltpu.CompilerParams(vmem_limit_bytes=24 * 2**20),
        cost_estimate=pl.CostEstimate(
            flops=2 * size**3, bytes_accessed=6 * size * size, transcendentals=0
        ),
        name="products",
    )(both)


def update_kernel(
    product, gating, gain, bias, weight, out_far, gains, biases, rows_of, out, sems
):
    channels, rows, tokens = product.shape
    pitch = ROWS + PAD
    steps = rows // ROWS
    def send(start):
        place = pl.ds(start, SEND)
        return pltpu.make_async_copy(out.at[place], out_far.at[place], sems.at[start // SEND])

    gains[...] = jnp.broadcast_to(gain[...], (tokens, channels)).T
    biases[...] = jnp.broadcast_to(bias[...], (tokens, channels)).T

    def body(step, carry):
        base = pl.multiple_of(step * ROWS, ROWS)
        load = lambda channel: product[channel, pl.ds(base, ROWS), :].astype(F32)
        first = load(0)
        total = jnp.zeros_like(first)
        spread = jnp.zeros_like(first)
        for channel in range(1, channels):
            offset = load(channel) - first
            total = total + offset
            spread = spread + offset * offset
        total = total * (1.0 / channels)
        center = first + total
        scale = lax.rsqrt(spread * (1.0 / channels) - total * total + EPS)
        for channel in range(channels):
            normed = (load(channel) - center) * scale
            normed = normed * gains[channel : channel + 1, :] + biases[channel : channel + 1, :]
            rows_of[pl.ds(channel * pitch, ROWS), :] = normed
        for row in range(ROWS):
            normed = rows_of[pl.ds(row, channels, stride=pitch), :].astype(BF16)
            projected = lax.dot_general(
                normed, weight[...], (((0,), (0,)), ((), ())), preferred_element_type=F32
            )
            out[base + row] = gating[base + row] * projected
            if row % SEND == SEND - 1:
                send(base + row + 1 - SEND).start()
        return carry

    lax.fori_loop(0, steps, body, 0)
    for start in range(0, rows, SEND):
        send(start).wait()


def update(product, gating, gain, bias, weight):
    channels, rows, tokens = product.shape
    return pl.pallas_call(
        update_kernel,
        in_specs=[pl.BlockSpec(memory_space=pltpu.VMEM)] * 5,
        out_specs=pl.BlockSpec(memory_space=pltpu.HBM),
        out_shape=jax.ShapeDtypeStruct((rows, tokens, channels), F32),
        scratch_shapes=[
            pltpu.VMEM((channels, tokens), F32),
            pltpu.VMEM((channels, tokens), F32),
            pltpu.VMEM((channels * (ROWS + PAD), tokens), F32),
            pltpu.VMEM((rows, tokens, channels), F32),
            pltpu.SemaphoreType.DMA((rows // SEND,)),
        ],
        compiler_params=pltpu.CompilerParams(vmem_limit_bytes=20 * 2**20),
        cost_estimate=pl.CostEstimate(
            flops=2 * rows * tokens * channels * channels,
            bytes_accessed=10 * rows * tokens * channels,
            transcendentals=0,
        ),
        name="update",
    )(product, gating, gain, bias, weight)


def per_device(n_rows, n_cols, pair, ln_gain, ln_bias, w_left, w_right, w_gate, w_out, out_gain, out_bias):
    rows, tokens, channels = pair.shape
    axes = ("row", "col")
    gain, bias = ln_gain[None], ln_bias[None]
    both, gating = edges(pair, gain, bias, w_left, w_right, w_gate)
    both = lax.all_to_all(both.reshape(channels, 2 * rows, tokens), axes, 0, 0, tiled=True)
    product = products(both.reshape(n_rows, n_cols, 2, rows, tokens)).reshape(channels, rows, tokens)
    product = lax.all_to_all(product, axes, 0, 0, tiled=True)
    return update(product, gating, out_gain[None], out_bias[None], w_out)


def solution(mesh):
    n_rows, n_cols = mesh.shape["row"], mesh.shape["col"]
    return jax.shard_map(
        lambda *args: per_device(n_rows, n_cols, *args),
        mesh=mesh,
        in_specs=(P("row", "col", None), P(), P(), P(), P(), P(), P(), P(), P()),
        out_specs=P("row", "col", None),
        check_vma=False,
    )
```

```python
import jax
import jax.numpy as jnp
from jax import lax
from jax.experimental import pallas as pl
from jax.experimental.pallas import tpu as pltpu
from jax.sharding import PartitionSpec as P

F32, BF16 = jnp.float32, jnp.bfloat16
EPS = 1e-05
ROWS = 16
BATCH = 4
SEND = 4
PAD = 4


def in_hbm(*arrays):
    return [pltpu.with_memory_space_constraint(array, pltpu.HBM) for array in arrays]


def edges_kernel(
    pair_far, gain_far, bias_far, left_far, right_far, gate_far, out, gating,
    pair, gain, bias, w_left, w_right, w_gate, weight, left_rows, right_rows, sems,
):
    rows, tokens, channels = pair.shape
    pitch = channels + PAD
    small = [
        pltpu.make_async_copy(far, near, sems.at[place])
        for place, (far, near) in enumerate(
            zip(
                (gain_far, bias_far, left_far, right_far, gate_far),
                (gain, bias, w_left, w_right, w_gate),
            )
        )
    ]

    def fetch(step):
        place = pl.ds(step * ROWS, ROWS)
        return pltpu.make_async_copy(pair_far.at[place], pair.at[place], sems.at[5 + step])

    fetch(0).start()
    for copy in small:
        copy.start()
    for step in range(1, rows // ROWS):
        fetch(step).start()
    for copy in small:
        copy.wait()
    weight[: 2 * channels] = w_left[...].T * 0.5
    weight[2 * channels :] = w_right[...].T * 0.5
    w_gate[...] = w_gate[...] * 0.5

    gains = jnp.broadcast_to(gain[...], (BATCH * tokens, channels)).T
    biases = jnp.broadcast_to(bias[...], (BATCH * tokens, channels)).T

    def body(step, carry):
        fetch(step).wait()
        base = pl.multiple_of(step * ROWS, ROWS)
        for row in range(0, ROWS, BATCH):
            values = pair[pl.ds(base + row, BATCH)].reshape(BATCH * tokens, channels).T
            center = jnp.sum(values, axis=0, keepdims=True) * (1.0 / channels)
            values = values - center
            spread = jnp.sum(values * values, axis=0, keepdims=True) * (1.0 / channels)
            normed = (values * lax.rsqrt(spread + EPS) * gains + biases).astype(BF16)
            projected = jnp.dot(weight[...], normed, preferred_element_type=F32)
            gates = lax.dot_general(
                normed, w_gate[...], (((0,), (0,)), ((), ())), preferred_element_type=F32
            )
            gating[pl.ds(base + row, BATCH)] = 0.5 * jnp.tanh(gates).reshape(BATCH, tokens, channels) + 0.5
            gate_left, left, gate_right, right = jnp.split(projected, 4, axis=0)
            lefts = (jnp.tanh(gate_left) + 1.0) * left
            rights = (jnp.tanh(gate_right) + 1.0) * right
            for part in range(BATCH):
                place = pl.ds((row + part) * pitch, channels)
                lanes = slice(part * tokens, (part + 1) * tokens)
                left_rows[place, :] = lefts[:, lanes]
                right_rows[place, :] = rights[:, lanes]
        for channel in range(channels):
            place = pl.ds(channel, ROWS, stride=pitch)
            out[channel, 0, pl.ds(base, ROWS), :] = left_rows[place, :].astype(BF16)
            out[channel, 1, pl.ds(base, ROWS), :] = right_rows[place, :].astype(BF16)
        return carry

    lax.fori_loop(0, rows // ROWS, body, 0)


def edges(pair, gain, bias, w_left, w_right, w_gate):
    rows, tokens, channels = pair.shape
    far = pl.BlockSpec(memory_space=pltpu.HBM)
    return pl.pallas_call(
        edges_kernel,
        in_specs=[far] * 6,
        out_specs=[pl.BlockSpec(memory_space=pltpu.VMEM)] * 2,
        out_shape=[
            jax.ShapeDtypeStruct((channels, 2, rows, tokens), BF16),
            jax.ShapeDtypeStruct(pair.shape, F32),
        ],
        scratch_shapes=[
            pltpu.VMEM(pair.shape, F32),
            pltpu.VMEM(gain.shape, F32),
            pltpu.VMEM(bias.shape, F32),
            pltpu.VMEM(w_left.shape, BF16),
            pltpu.VMEM(w_right.shape, BF16),
            pltpu.VMEM(w_gate.shape, BF16),
            pltpu.VMEM((4 * channels, channels), BF16),
            pltpu.VMEM((ROWS * (channels + PAD), tokens), F32),
            pltpu.VMEM((ROWS * (channels + PAD), tokens), F32),
            pltpu.SemaphoreType.DMA((5 + rows // ROWS,)),
        ],
        compiler_params=pltpu.CompilerParams(vmem_limit_bytes=20 * 2**20),
        cost_estimate=pl.CostEstimate(
            flops=10 * rows * tokens * channels * channels,
            bytes_accessed=12 * rows * tokens * channels,
            transcendentals=3 * rows * tokens * channels,
        ),
        name="edges",
    )(*in_hbm(pair, gain, bias, w_left, w_right, w_gate))


def product_kernel(both, out, left_turned, right_whole):
    n_rows, n_cols, _, depth, tokens = both.shape
    for col in range(n_cols):
        lanes = slice(col * tokens, (col + 1) * tokens)
        for row in range(n_rows):
            right_whole[row * depth : (row + 1) * depth, lanes] = both[row, col, 1]
        column = jnp.concatenate([both[row, col, 0] for row in range(n_rows)], axis=0)
        left_turned[lanes, :] = column.T
    for col in range(0, n_cols, 2):
        total = jnp.dot(
            left_turned[...],
            right_whole[:, col * tokens : (col + 2) * tokens],
            preferred_element_type=F32,
        ).astype(BF16)
        for part in range(2):
            block = total[:, part * tokens : (part + 1) * tokens]
            out[:, col + part] = block.reshape(n_rows, depth, tokens)


def products(both):
    n_rows, n_cols, _, depth, tokens = both.shape
    size = n_rows * depth
    return pl.pallas_call(
        product_kernel,
        out_shape=jax.ShapeDtypeStruct((n_rows, n_cols, depth, tokens), BF16),
        scratch_shapes=[pltpu.VMEM((size, size), BF16)] * 2,
        compiler_params=pltpu.CompilerParams(vmem_limit_bytes=24 * 2**20),
        cost_estimate=pl.CostEstimate(
            flops=2 * size**3, bytes_accessed=6 * size * size, transcendentals=0
        ),
        name="products",
    )(both)


def update_kernel(
    product, gating, gain, bias, weight, out_far, gains, biases, rows_of, out, sems
):
    channels, rows, tokens = product.shape
    pitch = ROWS + PAD
    steps = rows // ROWS
    def send(start):
        place = pl.ds(start, SEND)
        return pltpu.make_async_copy(out.at[place], out_far.at[place], sems.at[start // SEND])

    gains[...] = jnp.broadcast_to(gain[...], (tokens, channels)).T
    biases[...] = jnp.broadcast_to(bias[...], (tokens, channels)).T

    def body(step, carry):
        base = pl.multiple_of(step * ROWS, ROWS)
        for channel in range(channels):
            rows_of[pl.ds(channel * pitch, ROWS), :] = product[
                channel, pl.ds(base, ROWS), :
            ].astype(F32)
        for row in range(ROWS):
            values = rows_of[pl.ds(row, channels, stride=pitch), :]
            center = jnp.sum(values, axis=0, keepdims=True) * (1.0 / channels)
            values = values - center
            spread = jnp.sum(values * values, axis=0, keepdims=True) * (1.0 / channels)
            normed = (values * lax.rsqrt(spread + EPS) * gains[...] + biases[...]).astype(BF16)
            projected = lax.dot_general(
                normed, weight[...], (((0,), (0,)), ((), ())), preferred_element_type=F32
            )
            out[base + row] = gating[base + row] * projected
            if row % SEND == SEND - 1:
                send(base + row + 1 - SEND).start()
        return carry

    lax.fori_loop(0, steps, body, 0)
    for start in range(0, rows, SEND):
        send(start).wait()


def update(product, gating, gain, bias, weight):
    channels, rows, tokens = product.shape
    return pl.pallas_call(
        update_kernel,
        in_specs=[pl.BlockSpec(memory_space=pltpu.VMEM)] * 5,
        out_specs=pl.BlockSpec(memory_space=pltpu.HBM),
        out_shape=jax.ShapeDtypeStruct((rows, tokens, channels), F32),
        scratch_shapes=[
            pltpu.VMEM((channels, tokens), F32),
            pltpu.VMEM((channels, tokens), F32),
            pltpu.VMEM((channels * (ROWS + PAD), tokens), F32),
            pltpu.VMEM((rows, tokens, channels), F32),
            pltpu.SemaphoreType.DMA((rows // SEND,)),
        ],
        compiler_params=pltpu.CompilerParams(vmem_limit_bytes=20 * 2**20),
        cost_estimate=pl.CostEstimate(
            flops=2 * rows * tokens * channels * channels,
            bytes_accessed=10 * rows * tokens * channels,
            transcendentals=0,
        ),
        name="update",
    )(product, gating, gain, bias, weight)


def per_device(n_rows, n_cols, pair, ln_gain, ln_bias, w_left, w_right, w_gate, w_out, out_gain, out_bias):
    rows, tokens, channels = pair.shape
    axes = ("row", "col")
    gain, bias = ln_gain[None], ln_bias[None]
    both, gating = edges(pair, gain, bias, w_left, w_right, w_gate)
    both = lax.all_to_all(both.reshape(channels, 2 * rows, tokens), axes, 0, 0, tiled=True)
    product = products(both.reshape(n_rows, n_cols, 2, rows, tokens)).reshape(channels, rows, tokens)
    product = lax.all_to_all(product, axes, 0, 0, tiled=True)
    return update(product, gating, out_gain[None], out_bias[None], w_out)


def solution(mesh):
    n_rows, n_cols = mesh.shape["row"], mesh.shape["col"]
    return jax.shard_map(
        lambda *args: per_device(n_rows, n_cols, *args),
        mesh=mesh,
        in_specs=(P("row", "col", None), P(), P(), P(), P(), P(), P(), P(), P()),
        out_specs=P("row", "col", None),
        check_vma=False,
    )
```

```python
import jax
import jax.numpy as jnp
from jax import lax
from jax.experimental import pallas as pl
from jax.experimental.pallas import tpu as pltpu
from jax.sharding import PartitionSpec as P

F32, BF16 = jnp.float32, jnp.bfloat16
EPS = 1e-05
CHUNK = 32
ROWS = 16
BATCH = 4
SEND = 4
PAD = 4


def in_hbm(*arrays):
    return [pltpu.with_memory_space_constraint(array, pltpu.HBM) for array in arrays]


def edges_kernel(
    pair_far, gain_far, bias_far, left_far, right_far, gate_far, out, gating,
    pair, gain, bias, w_left, w_right, w_gate, weight, left_rows, right_rows, sems,
):
    rows, tokens, channels = pair.shape
    pitch = channels + PAD
    small = [
        pltpu.make_async_copy(far, near, sems.at[place])
        for place, (far, near) in enumerate(
            zip(
                (gain_far, bias_far, left_far, right_far, gate_far),
                (gain, bias, w_left, w_right, w_gate),
            )
        )
    ]

    def fetch(step):
        place = pl.ds(step * CHUNK, CHUNK)
        return pltpu.make_async_copy(pair_far.at[place], pair.at[place], sems.at[5 + step])

    fetch(0).start()
    for copy in small:
        copy.start()
    for step in range(1, rows // CHUNK):
        fetch(step).start()
    for copy in small:
        copy.wait()
    weight[: 2 * channels] = w_left[...].T * 0.5
    weight[2 * channels :] = w_right[...].T * 0.5
    w_gate[...] = w_gate[...] * 0.5

    gains = jnp.broadcast_to(gain[...], (BATCH * tokens, channels)).T
    biases = jnp.broadcast_to(bias[...], (BATCH * tokens, channels)).T

    def body(step, carry):
        fetch(step).wait()
        base = pl.multiple_of(step * CHUNK, CHUNK)
        for row in range(0, CHUNK, BATCH):
            values = pair[pl.ds(base + row, BATCH)].reshape(BATCH * tokens, channels).T
            center = jnp.sum(values, axis=0, keepdims=True) * (1.0 / channels)
            values = values - center
            spread = jnp.sum(values * values, axis=0, keepdims=True) * (1.0 / channels)
            normed = (values * lax.rsqrt(spread + EPS) * gains + biases).astype(BF16)
            projected = jnp.dot(weight[...], normed, preferred_element_type=F32)
            gates = lax.dot_general(
                normed, w_gate[...], (((0,), (0,)), ((), ())), preferred_element_type=F32
            )
            gating[pl.ds(base + row, BATCH)] = 0.5 * jnp.tanh(gates).reshape(BATCH, tokens, channels) + 0.5
            gate_left, left, gate_right, right = jnp.split(projected, 4, axis=0)
            lefts = (jnp.tanh(gate_left) + 1.0) * left
            rights = (jnp.tanh(gate_right) + 1.0) * right
            for part in range(BATCH):
                place = pl.ds((row + part) * pitch, channels)
                lanes = slice(part * tokens, (part + 1) * tokens)
                left_rows[place, :] = lefts[:, lanes]
                right_rows[place, :] = rights[:, lanes]
        for channel in range(channels):
            place = pl.ds(channel, CHUNK, stride=pitch)
            out[channel, 0, pl.ds(base, CHUNK), :] = left_rows[place, :].astype(BF16)
            out[channel, 1, pl.ds(base, CHUNK), :] = right_rows[place, :].astype(BF16)
        return carry

    lax.fori_loop(0, rows // CHUNK, body, 0)


def edges(pair, gain, bias, w_left, w_right, w_gate):
    rows, tokens, channels = pair.shape
    far = pl.BlockSpec(memory_space=pltpu.HBM)
    return pl.pallas_call(
        edges_kernel,
        in_specs=[far] * 6,
        out_specs=[pl.BlockSpec(memory_space=pltpu.VMEM)] * 2,
        out_shape=[
            jax.ShapeDtypeStruct((channels, 2, rows, tokens), BF16),
            jax.ShapeDtypeStruct(pair.shape, F32),
        ],
        scratch_shapes=[
            pltpu.VMEM(pair.shape, F32),
            pltpu.VMEM(gain.shape, F32),
            pltpu.VMEM(bias.shape, F32),
            pltpu.VMEM(w_left.shape, BF16),
            pltpu.VMEM(w_right.shape, BF16),
            pltpu.VMEM(w_gate.shape, BF16),
            pltpu.VMEM((4 * channels, channels), BF16),
            pltpu.VMEM((CHUNK * (channels + PAD), tokens), F32),
            pltpu.VMEM((CHUNK * (channels + PAD), tokens), F32),
            pltpu.SemaphoreType.DMA((5 + rows // CHUNK,)),
        ],
        compiler_params=pltpu.CompilerParams(vmem_limit_bytes=20 * 2**20),
        cost_estimate=pl.CostEstimate(
            flops=10 * rows * tokens * channels * channels,
            bytes_accessed=12 * rows * tokens * channels,
            transcendentals=3 * rows * tokens * channels,
        ),
        name="edges",
    )(*in_hbm(pair, gain, bias, w_left, w_right, w_gate))


def product_kernel(both, out, left_turned):
    n_rows, n_cols, _, depth, tokens = both.shape

    def column(col, side):
        return jnp.concatenate([both[row, col, side] for row in range(n_rows)], axis=0)

    for col in range(n_cols):
        left_turned[col * tokens : (col + 1) * tokens, :] = column(col, 0).T
    for col in range(0, n_cols, 2):
        rights = jnp.concatenate([column(col, 1), column(col + 1, 1)], axis=1)
        total = jnp.dot(left_turned[...], rights, preferred_element_type=F32).astype(BF16)
        for part in range(2):
            block = total[:, part * tokens : (part + 1) * tokens]
            out[:, col + part] = block.reshape(n_rows, depth, tokens)


def products(both):
    n_rows, n_cols, _, depth, tokens = both.shape
    size = n_rows * depth
    return pl.pallas_call(
        product_kernel,
        out_shape=jax.ShapeDtypeStruct((n_rows, n_cols, depth, tokens), BF16),
        scratch_shapes=[pltpu.VMEM((size, size), BF16)],
        compiler_params=pltpu.CompilerParams(vmem_limit_bytes=24 * 2**20),
        cost_estimate=pl.CostEstimate(
            flops=2 * size**3, bytes_accessed=6 * size * size, transcendentals=0
        ),
        name="products",
    )(both)


def update_kernel(
    product, gating, gain, bias, weight, out_far, gains, biases, rows_of, out, sems
):
    channels, rows, tokens = product.shape
    pitch = ROWS + PAD
    steps = rows // ROWS
    def send(start):
        place = pl.ds(start, SEND)
        return pltpu.make_async_copy(out.at[place], out_far.at[place], sems.at[start // SEND])

    gains[...] = jnp.broadcast_to(gain[...], (tokens, channels)).T
    biases[...] = jnp.broadcast_to(bias[...], (tokens, channels)).T

    def body(step, carry):
        base = pl.multiple_of(step * ROWS, ROWS)
        for channel in range(channels):
            rows_of[pl.ds(channel * pitch, ROWS), :] = product[
                channel, pl.ds(base, ROWS), :
            ].astype(F32)
        for row in range(ROWS):
            values = rows_of[pl.ds(row, channels, stride=pitch), :]
            center = jnp.sum(values, axis=0, keepdims=True) * (1.0 / channels)
            values = values - center
            spread = jnp.sum(values * values, axis=0, keepdims=True) * (1.0 / channels)
            normed = (values * lax.rsqrt(spread + EPS) * gains[...] + biases[...]).astype(BF16)
            projected = lax.dot_general(
                normed, weight[...], (((0,), (0,)), ((), ())), preferred_element_type=F32
            )
            out[base + row] = gating[base + row] * projected
            if row % SEND == SEND - 1:
                send(base + row + 1 - SEND).start()
        return carry

    lax.fori_loop(0, steps, body, 0, unroll=True)
    for start in range(0, rows, SEND):
        send(start).wait()


def update(product, gating, gain, bias, weight):
    channels, rows, tokens = product.shape
    return pl.pallas_call(
        update_kernel,
        in_specs=[pl.BlockSpec(memory_space=pltpu.VMEM)] * 5,
        out_specs=pl.BlockSpec(memory_space=pltpu.HBM),
        out_shape=jax.ShapeDtypeStruct((rows, tokens, channels), F32),
        scratch_shapes=[
            pltpu.VMEM((channels, tokens), F32),
            pltpu.VMEM((channels, tokens), F32),
            pltpu.VMEM((channels * (ROWS + PAD), tokens), F32),
            pltpu.VMEM((rows, tokens, channels), F32),
            pltpu.SemaphoreType.DMA((rows // SEND,)),
        ],
        compiler_params=pltpu.CompilerParams(vmem_limit_bytes=20 * 2**20),
        cost_estimate=pl.CostEstimate(
            flops=2 * rows * tokens * channels * channels,
            bytes_accessed=10 * rows * tokens * channels,
            transcendentals=0,
        ),
        name="update",
    )(product, gating, gain, bias, weight)


def per_device(n_rows, n_cols, pair, ln_gain, ln_bias, w_left, w_right, w_gate, w_out, out_gain, out_bias):
    rows, tokens, channels = pair.shape
    axes = ("row", "col")
    gain, bias = ln_gain[None], ln_bias[None]
    both, gating = edges(pair, gain, bias, w_left, w_right, w_gate)
    both = lax.all_to_all(both.reshape(channels, 2 * rows, tokens), axes, 0, 0, tiled=True)
    product = products(both.reshape(n_rows, n_cols, 2, rows, tokens)).reshape(channels, rows, tokens)
    product = lax.all_to_all(product, axes, 0, 0, tiled=True)
    return update(product, gating, out_gain[None], out_bias[None], w_out)


def solution(mesh):
    n_rows, n_cols = mesh.shape["row"], mesh.shape["col"]
    return jax.shard_map(
        lambda *args: per_device(n_rows, n_cols, *args),
        mesh=mesh,
        in_specs=(P("row", "col", None), P(), P(), P(), P(), P(), P(), P(), P()),
        out_specs=P("row", "col", None),
        check_vma=False,
    )
```

```python
import jax
import jax.numpy as jnp
from jax import lax
from jax.experimental import pallas as pl
from jax.experimental.pallas import tpu as pltpu
from jax.sharding import PartitionSpec as P

F32, BF16 = jnp.float32, jnp.bfloat16
EPS = 1e-05
FIRST = 16
ROWS = 16
BATCH = 4
SEND = 4
PAD = 4


def in_hbm(*arrays):
    return [pltpu.with_memory_space_constraint(array, pltpu.HBM) for array in arrays]


def edges_kernel(
    pair_far, gain_far, bias_far, left_far, right_far, gate_far, out, gating,
    pair, gain, bias, w_left, w_right, w_gate, weight, left_rows, right_rows, sems,
):
    rows, tokens, channels = pair.shape
    pitch = channels + PAD
    small = [
        pltpu.make_async_copy(far, near, sems.at[place])
        for place, (far, near) in enumerate(
            zip(
                (gain_far, bias_far, left_far, right_far, gate_far),
                (gain, bias, w_left, w_right, w_gate),
            )
        )
    ]

    steps = [(0, FIRST), (FIRST, rows)]
    fetches = [
        pltpu.make_async_copy(
            pair_far.at[pl.ds(start, stop - start)],
            pair.at[pl.ds(start, stop - start)],
            sems.at[5 + step],
        )
        for step, (start, stop) in enumerate(steps)
    ]
    fetches[0].start()
    for copy in small:
        copy.start()
    fetches[1].start()
    for copy in small:
        copy.wait()
    weight[: 2 * channels] = w_left[...].T * 0.5
    weight[2 * channels :] = w_right[...].T * 0.5
    w_gate[...] = w_gate[...] * 0.5

    gains = jnp.broadcast_to(gain[...], (BATCH * tokens, channels)).T
    biases = jnp.broadcast_to(bias[...], (BATCH * tokens, channels)).T

    for copy, (start, stop) in zip(fetches, steps):
        copy.wait()
        for row in range(start, stop, BATCH):
            values = pair[pl.ds(row, BATCH)].reshape(BATCH * tokens, channels).T
            center = jnp.sum(values, axis=0, keepdims=True) * (1.0 / channels)
            values = values - center
            spread = jnp.sum(values * values, axis=0, keepdims=True) * (1.0 / channels)
            normed = (values * lax.rsqrt(spread + EPS) * gains + biases).astype(BF16)
            projected = jnp.dot(weight[...], normed, preferred_element_type=F32)
            gates = lax.dot_general(
                normed, w_gate[...], (((0,), (0,)), ((), ())), preferred_element_type=F32
            )
            gating[pl.ds(row, BATCH)] = 0.5 * jnp.tanh(gates).reshape(BATCH, tokens, channels) + 0.5
            gate_left, left, gate_right, right = jnp.split(projected, 4, axis=0)
            lefts = (jnp.tanh(gate_left) + 1.0) * left
            rights = (jnp.tanh(gate_right) + 1.0) * right
            for part in range(BATCH):
                place = pl.ds((row + part) * pitch, channels)
                lanes = slice(part * tokens, (part + 1) * tokens)
                left_rows[place, :] = lefts[:, lanes]
                right_rows[place, :] = rights[:, lanes]
        for channel in range(channels):
            place = pl.ds(start * pitch + channel, stop - start, stride=pitch)
            out[channel, 0, start:stop, :] = left_rows[place, :].astype(BF16)
            out[channel, 1, start:stop, :] = right_rows[place, :].astype(BF16)


def edges(pair, gain, bias, w_left, w_right, w_gate):
    rows, tokens, channels = pair.shape
    far = pl.BlockSpec(memory_space=pltpu.HBM)
    return pl.pallas_call(
        edges_kernel,
        in_specs=[far] * 6,
        out_specs=[pl.BlockSpec(memory_space=pltpu.VMEM)] * 2,
        out_shape=[
            jax.ShapeDtypeStruct((channels, 2, rows, tokens), BF16),
            jax.ShapeDtypeStruct(pair.shape, F32),
        ],
        scratch_shapes=[
            pltpu.VMEM(pair.shape, F32),
            pltpu.VMEM(gain.shape, F32),
            pltpu.VMEM(bias.shape, F32),
            pltpu.VMEM(w_left.shape, BF16),
            pltpu.VMEM(w_right.shape, BF16),
            pltpu.VMEM(w_gate.shape, BF16),
            pltpu.VMEM((4 * channels, channels), BF16),
            pltpu.VMEM((rows * (channels + PAD), tokens), F32),
            pltpu.VMEM((rows * (channels + PAD), tokens), F32),
            pltpu.SemaphoreType.DMA((7,)),
        ],
        compiler_params=pltpu.CompilerParams(vmem_limit_bytes=28 * 2**20),
        cost_estimate=pl.CostEstimate(
            flops=10 * rows * tokens * channels * channels,
            bytes_accessed=12 * rows * tokens * channels,
            transcendentals=3 * rows * tokens * channels,
        ),
        name="edges",
    )(*in_hbm(pair, gain, bias, w_left, w_right, w_gate))


def product_kernel(both, out, left_turned):
    n_rows, n_cols, _, depth, tokens = both.shape

    def column(col, side):
        return jnp.concatenate([both[row, col, side] for row in range(n_rows)], axis=0)

    for col in range(n_cols):
        left_turned[col * tokens : (col + 1) * tokens, :] = column(col, 0).T
    for col in range(0, n_cols, 2):
        rights = jnp.concatenate([column(col, 1), column(col + 1, 1)], axis=1)
        total = jnp.dot(left_turned[...], rights, preferred_element_type=F32).astype(BF16)
        for part in range(2):
            block = total[:, part * tokens : (part + 1) * tokens]
            out[:, col + part] = block.reshape(n_rows, depth, tokens)


def products(both):
    n_rows, n_cols, _, depth, tokens = both.shape
    size = n_rows * depth
    return pl.pallas_call(
        product_kernel,
        out_shape=jax.ShapeDtypeStruct((n_rows, n_cols, depth, tokens), BF16),
        scratch_shapes=[pltpu.VMEM((size, size), BF16)],
        compiler_params=pltpu.CompilerParams(vmem_limit_bytes=24 * 2**20),
        cost_estimate=pl.CostEstimate(
            flops=2 * size**3, bytes_accessed=6 * size * size, transcendentals=0
        ),
        name="products",
    )(both)


def update_kernel(
    product, gating, gain, bias, weight, out_far, gains, biases, rows_of, out, sems
):
    channels, rows, tokens = product.shape
    pitch = ROWS + PAD
    steps = rows // ROWS
    def send(start):
        place = pl.ds(start, SEND)
        return pltpu.make_async_copy(out.at[place], out_far.at[place], sems.at[start // SEND])

    gains[...] = jnp.broadcast_to(gain[...], (tokens, channels)).T
    biases[...] = jnp.broadcast_to(bias[...], (tokens, channels)).T

    def body(step, carry):
        base = pl.multiple_of(step * ROWS, ROWS)
        for channel in range(channels):
            rows_of[pl.ds(channel * pitch, ROWS), :] = product[
                channel, pl.ds(base, ROWS), :
            ].astype(F32)
        for row in range(ROWS):
            values = rows_of[pl.ds(row, channels, stride=pitch), :]
            center = jnp.sum(values, axis=0, keepdims=True) * (1.0 / channels)
            values = values - center
            spread = jnp.sum(values * values, axis=0, keepdims=True) * (1.0 / channels)
            normed = (values * lax.rsqrt(spread + EPS) * gains[...] + biases[...]).astype(BF16)
            projected = lax.dot_general(
                normed, weight[...], (((0,), (0,)), ((), ())), preferred_element_type=F32
            )
            out[base + row] = gating[base + row] * projected
            if row % SEND == SEND - 1:
                send(base + row + 1 - SEND).start()
        return carry

    lax.fori_loop(0, steps, body, 0, unroll=True)
    for start in range(0, rows, SEND):
        send(start).wait()


def update(product, gating, gain, bias, weight):
    channels, rows, tokens = product.shape
    return pl.pallas_call(
        update_kernel,
        in_specs=[pl.BlockSpec(memory_space=pltpu.VMEM)] * 5,
        out_specs=pl.BlockSpec(memory_space=pltpu.HBM),
        out_shape=jax.ShapeDtypeStruct((rows, tokens, channels), F32),
        scratch_shapes=[
            pltpu.VMEM((channels, tokens), F32),
            pltpu.VMEM((channels, tokens), F32),
            pltpu.VMEM((channels * (ROWS + PAD), tokens), F32),
            pltpu.VMEM((rows, tokens, channels), F32),
            pltpu.SemaphoreType.DMA((rows // SEND,)),
        ],
        compiler_params=pltpu.CompilerParams(vmem_limit_bytes=20 * 2**20),
        cost_estimate=pl.CostEstimate(
            flops=2 * rows * tokens * channels * channels,
            bytes_accessed=10 * rows * tokens * channels,
            transcendentals=0,
        ),
        name="update",
    )(product, gating, gain, bias, weight)


def per_device(n_rows, n_cols, pair, ln_gain, ln_bias, w_left, w_right, w_gate, w_out, out_gain, out_bias):
    rows, tokens, channels = pair.shape
    axes = ("row", "col")
    gain, bias = ln_gain[None], ln_bias[None]
    both, gating = edges(pair, gain, bias, w_left, w_right, w_gate)
    both = lax.all_to_all(both.reshape(channels, 2 * rows, tokens), axes, 0, 0, tiled=True)
    product = products(both.reshape(n_rows, n_cols, 2, rows, tokens)).reshape(channels, rows, tokens)
    product = lax.all_to_all(product, axes, 0, 0, tiled=True)
    return update(product, gating, out_gain[None], out_bias[None], w_out)


def solution(mesh):
    n_rows, n_cols = mesh.shape["row"], mesh.shape["col"]
    return jax.shard_map(
        lambda *args: per_device(n_rows, n_cols, *args),
        mesh=mesh,
        in_specs=(P("row", "col", None), P(), P(), P(), P(), P(), P(), P(), P()),
        out_specs=P("row", "col", None),
        check_vma=False,
    )
```

```python
import jax
import jax.numpy as jnp
from jax import lax
from jax.experimental import pallas as pl
from jax.experimental.pallas import tpu as pltpu
from jax.sharding import PartitionSpec as P

F32, BF16 = jnp.float32, jnp.bfloat16
EPS = 1e-05
FIRST = 16
ROWS = 16
BATCH = 4
SEND = 4
PAD = 4


def in_hbm(*arrays):
    return [pltpu.with_memory_space_constraint(array, pltpu.HBM) for array in arrays]


def edges_kernel(
    pair_far, gain_far, bias_far, left_far, right_far, out,
    pair, gain, bias, w_left, w_right, weight, left_rows, right_rows, sems,
):
    rows, tokens, channels = pair.shape
    pitch = channels + PAD
    small = [
        pltpu.make_async_copy(far, near, sems.at[place])
        for place, (far, near) in enumerate(
            zip(
                (gain_far, bias_far, left_far, right_far),
                (gain, bias, w_left, w_right),
            )
        )
    ]

    steps = [(0, FIRST), (FIRST, rows)]
    fetches = [
        pltpu.make_async_copy(
            pair_far.at[pl.ds(start, stop - start)],
            pair.at[pl.ds(start, stop - start)],
            sems.at[4 + step],
        )
        for step, (start, stop) in enumerate(steps)
    ]
    fetches[0].start()
    for copy in small:
        copy.start()
    fetches[1].start()
    for copy in small:
        copy.wait()
    weight[: 2 * channels] = w_left[...].T * 0.5
    weight[2 * channels :] = w_right[...].T * 0.5

    gains = jnp.broadcast_to(gain[...], (BATCH * tokens, channels)).T
    biases = jnp.broadcast_to(bias[...], (BATCH * tokens, channels)).T

    for copy, (start, stop) in zip(fetches, steps):
        copy.wait()
        for row in range(start, stop, BATCH):
            values = pair[pl.ds(row, BATCH)].reshape(BATCH * tokens, channels).T
            center = jnp.sum(values, axis=0, keepdims=True) * (1.0 / channels)
            values = values - center
            spread = jnp.sum(values * values, axis=0, keepdims=True) * (1.0 / channels)
            normed = (values * lax.rsqrt(spread + EPS) * gains + biases).astype(BF16)
            projected = jnp.dot(weight[...], normed, preferred_element_type=F32)
            gate_left, left, gate_right, right = jnp.split(projected, 4, axis=0)
            lefts = (jnp.tanh(gate_left) + 1.0) * left
            rights = (jnp.tanh(gate_right) + 1.0) * right
            for part in range(BATCH):
                place = pl.ds((row + part) * pitch, channels)
                lanes = slice(part * tokens, (part + 1) * tokens)
                left_rows[place, :] = lefts[:, lanes]
                right_rows[place, :] = rights[:, lanes]
        for channel in range(channels):
            place = pl.ds(start * pitch + channel, stop - start, stride=pitch)
            out[channel, 0, start:stop, :] = left_rows[place, :].astype(BF16)
            out[channel, 1, start:stop, :] = right_rows[place, :].astype(BF16)


def edges(pair, gain, bias, w_left, w_right):
    rows, tokens, channels = pair.shape
    far = pl.BlockSpec(memory_space=pltpu.HBM)
    return pl.pallas_call(
        edges_kernel,
        in_specs=[far] * 5,
        out_specs=pl.BlockSpec(memory_space=pltpu.VMEM),
        out_shape=jax.ShapeDtypeStruct((channels, 2, rows, tokens), BF16),
        scratch_shapes=[
            pltpu.VMEM(pair.shape, F32),
            pltpu.VMEM(gain.shape, F32),
            pltpu.VMEM(bias.shape, F32),
            pltpu.VMEM(w_left.shape, BF16),
            pltpu.VMEM(w_right.shape, BF16),
            pltpu.VMEM((4 * channels, channels), BF16),
            pltpu.VMEM((rows * (channels + PAD), tokens), F32),
            pltpu.VMEM((rows * (channels + PAD), tokens), F32),
            pltpu.SemaphoreType.DMA((6,)),
        ],
        compiler_params=pltpu.CompilerParams(vmem_limit_bytes=28 * 2**20),
        cost_estimate=pl.CostEstimate(
            flops=8 * rows * tokens * channels * channels,
            bytes_accessed=8 * rows * tokens * channels,
            transcendentals=2 * rows * tokens * channels,
        ),
        name="edges",
    )(*in_hbm(pair, gain, bias, w_left, w_right))


def gating_kernel(pair, gain, bias, weight, gating):
    rows, tokens, channels = pair.shape
    values = pair[...].reshape(rows * tokens, channels)
    center = jnp.mean(values, axis=-1, keepdims=True)
    values = values - center
    spread = jnp.mean(values * values, axis=-1, keepdims=True)
    normed = (values * lax.rsqrt(spread + EPS) * gain[...] + bias[...]).astype(BF16)
    projected = jnp.dot(normed, weight[...], preferred_element_type=F32)
    gating[...] = (0.5 * jnp.tanh(0.5 * projected) + 0.5).reshape(rows, tokens, channels)


def gates(pair, gain, bias, weight):
    rows, tokens, channels = pair.shape
    whole = lambda *shape: pl.BlockSpec(shape, lambda step: (0,) * len(shape))
    block = pl.BlockSpec((ROWS, tokens, channels), lambda step: (step, 0, 0))
    return pl.pallas_call(
        gating_kernel,
        grid=(rows // ROWS,),
        in_specs=[block, whole(1, channels), whole(1, channels), whole(channels, channels)],
        out_specs=block,
        out_shape=pltpu.VMEM(pair.shape, F32),
        compiler_params=pltpu.CompilerParams(vmem_limit_bytes=16 * 2**20),
        cost_estimate=pl.CostEstimate(
            flops=2 * rows * tokens * channels * channels,
            bytes_accessed=8 * rows * tokens * channels,
            transcendentals=rows * tokens * channels,
        ),
        name="gates",
    )(pair, gain, bias, weight)


def product_kernel(both, out_far, left_turned, out, sems):
    n_rows, n_cols, _, depth, tokens = both.shape

    def column(col, side):
        return jnp.concatenate([both[row, col, side] for row in range(n_rows)], axis=0)

    for col in range(n_cols):
        left_turned[col * tokens : (col + 1) * tokens, :] = column(col, 0).T
    copies = []
    for col in range(0, n_cols, 2):
        rights = jnp.concatenate([column(col, 1), column(col + 1, 1)], axis=1)
        total = jnp.dot(left_turned[...], rights, preferred_element_type=F32).astype(BF16)
        for part in range(2):
            block = total[:, part * tokens : (part + 1) * tokens]
            out[:, col + part] = block.reshape(n_rows, depth, tokens)
        place = pl.ds(col, 2)
        copies.append(
            pltpu.make_async_copy(out.at[:, place], out_far.at[:, place], sems.at[col // 2])
        )
        copies[-1].start()
    for copy in copies:
        copy.wait()


def products(both):
    n_rows, n_cols, _, depth, tokens = both.shape
    size = n_rows * depth
    return pl.pallas_call(
        product_kernel,
        in_specs=[pl.BlockSpec(memory_space=pltpu.VMEM)],
        out_specs=pl.BlockSpec(memory_space=pltpu.HBM),
        out_shape=pltpu.HBM((n_rows, n_cols, depth, tokens), BF16),
        scratch_shapes=[
            pltpu.VMEM((size, size), BF16),
            pltpu.VMEM((n_rows, n_cols, depth, tokens), BF16),
            pltpu.SemaphoreType.DMA((n_cols // 2,)),
        ],
        compiler_params=pltpu.CompilerParams(vmem_limit_bytes=24 * 2**20),
        cost_estimate=pl.CostEstimate(
            flops=2 * size**3, bytes_accessed=6 * size * size, transcendentals=0
        ),
        name="products",
    )(both)


def update_kernel(
    product, gating, gain, bias, weight, out_far, gains, biases, rows_of, out, sems
):
    channels, rows, tokens = product.shape
    pitch = ROWS + PAD
    steps = rows // ROWS
    def send(start):
        place = pl.ds(start, SEND)
        return pltpu.make_async_copy(out.at[place], out_far.at[place], sems.at[start // SEND])

    gains[...] = jnp.broadcast_to(gain[...], (tokens, channels)).T
    biases[...] = jnp.broadcast_to(bias[...], (tokens, channels)).T

    def body(step, carry):
        base = pl.multiple_of(step * ROWS, ROWS)
        for channel in range(channels):
            rows_of[pl.ds(channel * pitch, ROWS), :] = product[
                channel, pl.ds(base, ROWS), :
            ].astype(F32)
        for row in range(ROWS):
            values = rows_of[pl.ds(row, channels, stride=pitch), :]
            center = jnp.sum(values, axis=0, keepdims=True) * (1.0 / channels)
            values = values - center
            spread = jnp.sum(values * values, axis=0, keepdims=True) * (1.0 / channels)
            normed = (values * lax.rsqrt(spread + EPS) * gains[...] + biases[...]).astype(BF16)
            projected = lax.dot_general(
                normed, weight[...], (((0,), (0,)), ((), ())), preferred_element_type=F32
            )
            out[base + row] = gating[base + row] * projected
            if row % SEND == SEND - 1:
                send(base + row + 1 - SEND).start()
        return carry

    lax.fori_loop(0, steps, body, 0, unroll=True)
    for start in range(0, rows, SEND):
        send(start).wait()


def update(product, gating, gain, bias, weight):
    channels, rows, tokens = product.shape
    return pl.pallas_call(
        update_kernel,
        in_specs=[pl.BlockSpec(memory_space=pltpu.VMEM)] * 5,
        out_specs=pl.BlockSpec(memory_space=pltpu.HBM),
        out_shape=jax.ShapeDtypeStruct((rows, tokens, channels), F32),
        scratch_shapes=[
            pltpu.VMEM((channels, tokens), F32),
            pltpu.VMEM((channels, tokens), F32),
            pltpu.VMEM((channels * (ROWS + PAD), tokens), F32),
            pltpu.VMEM((rows, tokens, channels), F32),
            pltpu.SemaphoreType.DMA((rows // SEND,)),
        ],
        compiler_params=pltpu.CompilerParams(vmem_limit_bytes=20 * 2**20),
        cost_estimate=pl.CostEstimate(
            flops=2 * rows * tokens * channels * channels,
            bytes_accessed=10 * rows * tokens * channels,
            transcendentals=0,
        ),
        name="update",
    )(product, gating, gain, bias, weight)


def per_device(n_rows, n_cols, pair, ln_gain, ln_bias, w_left, w_right, w_gate, w_out, out_gain, out_bias):
    rows, tokens, channels = pair.shape
    axes = ("row", "col")
    gain, bias = ln_gain[None], ln_bias[None]
    both = edges(pair, gain, bias, w_left, w_right)
    gating = gates(pair, gain, bias, w_gate)
    both = lax.all_to_all(both.reshape(channels, 2 * rows, tokens), axes, 0, 0, tiled=True)
    product = products(both.reshape(n_rows, n_cols, 2, rows, tokens)).reshape(channels, rows, tokens)
    product = lax.all_to_all(product, axes, 0, 0, tiled=True)
    return update(product, gating, out_gain[None], out_bias[None], w_out)


def solution(mesh):
    n_rows, n_cols = mesh.shape["row"], mesh.shape["col"]
    return jax.shard_map(
        lambda *args: per_device(n_rows, n_cols, *args),
        mesh=mesh,
        in_specs=(P("row", "col", None), P(), P(), P(), P(), P(), P(), P(), P()),
        out_specs=P("row", "col", None),
        check_vma=False,
    )
```

```python
import jax
import jax.numpy as jnp
from jax import lax
from jax.experimental import pallas as pl
from jax.experimental.pallas import tpu as pltpu
from jax.sharding import PartitionSpec as P

F32, BF16 = jnp.float32, jnp.bfloat16
EPS = 1e-05
FIRST = 16
ROWS = 16
BATCH = 4
SEND = 4
PAD = 4


def in_hbm(*arrays):
    return [pltpu.with_memory_space_constraint(array, pltpu.HBM) for array in arrays]


def edges_kernel(
    pair_far, gain_far, bias_far, left_far, right_far, gate_far, out, gating,
    pair, gain, bias, w_left, w_right, w_gate, weight, left_rows, right_rows, sems,
):
    rows, tokens, channels = pair.shape
    pitch = channels + PAD
    small = [
        pltpu.make_async_copy(far, near, sems.at[place])
        for place, (far, near) in enumerate(
            zip(
                (gain_far, bias_far, left_far, right_far, gate_far),
                (gain, bias, w_left, w_right, w_gate),
            )
        )
    ]

    steps = [(0, FIRST), (FIRST, rows)]
    fetches = [
        pltpu.make_async_copy(
            pair_far.at[pl.ds(start, stop - start)],
            pair.at[pl.ds(start, stop - start)],
            sems.at[5 + step],
        )
        for step, (start, stop) in enumerate(steps)
    ]
    fetches[0].start()
    for copy in small:
        copy.start()
    fetches[1].start()
    for copy in small[:2]:
        copy.wait()
    gains = jnp.broadcast_to(gain[...], (BATCH * tokens, channels)).T
    biases = jnp.broadcast_to(bias[...], (BATCH * tokens, channels)).T

    fetches[0].wait()
    for copy in small[2:]:
        copy.wait()
    weight[: 2 * channels] = w_left[...].T * 0.5
    weight[2 * channels :] = w_right[...].T * 0.5
    w_gate[...] = w_gate[...] * 0.5

    for copy, (start, stop) in zip(fetches, steps):
        if start > 0:
            copy.wait()
        for row in range(start, stop, BATCH):
            values = pair[pl.ds(row, BATCH)].reshape(BATCH * tokens, channels).T
            center = jnp.sum(values, axis=0, keepdims=True) * (1.0 / channels)
            values = values - center
            spread = jnp.sum(values * values, axis=0, keepdims=True) * (1.0 / channels)
            normed = (values * lax.rsqrt(spread + EPS) * gains + biases).astype(BF16)
            projected = jnp.dot(weight[...], normed, preferred_element_type=F32)
            gates = lax.dot_general(
                normed, w_gate[...], (((0,), (0,)), ((), ())), preferred_element_type=F32
            )
            gating[pl.ds(row, BATCH)] = 0.5 * jnp.tanh(gates).reshape(BATCH, tokens, channels) + 0.5
            gate_left, left, gate_right, right = jnp.split(projected, 4, axis=0)
            lefts = (jnp.tanh(gate_left) + 1.0) * left
            rights = (jnp.tanh(gate_right) + 1.0) * right
            for part in range(BATCH):
                place = pl.ds((row + part) * pitch, channels)
                lanes = slice(part * tokens, (part + 1) * tokens)
                left_rows[place, :] = lefts[:, lanes]
                right_rows[place, :] = rights[:, lanes]
        for channel in range(channels):
            place = pl.ds(start * pitch + channel, stop - start, stride=pitch)
            out[channel, 0, start:stop, :] = left_rows[place, :].astype(BF16)
            out[channel, 1, start:stop, :] = right_rows[place, :].astype(BF16)


def edges(pair, gain, bias, w_left, w_right, w_gate):
    rows, tokens, channels = pair.shape
    far = pl.BlockSpec(memory_space=pltpu.HBM)
    return pl.pallas_call(
        edges_kernel,
        in_specs=[far] * 6,
        out_specs=[pl.BlockSpec(memory_space=pltpu.VMEM)] * 2,
        out_shape=[
            jax.ShapeDtypeStruct((channels, 2, rows, tokens), BF16),
            jax.ShapeDtypeStruct(pair.shape, F32),
        ],
        scratch_shapes=[
            pltpu.VMEM(pair.shape, F32),
            pltpu.VMEM(gain.shape, F32),
            pltpu.VMEM(bias.shape, F32),
            pltpu.VMEM(w_left.shape, BF16),
            pltpu.VMEM(w_right.shape, BF16),
            pltpu.VMEM(w_gate.shape, BF16),
            pltpu.VMEM((4 * channels, channels), BF16),
            pltpu.VMEM((rows * (channels + PAD), tokens), F32),
            pltpu.VMEM((rows * (channels + PAD), tokens), F32),
            pltpu.SemaphoreType.DMA((7,)),
        ],
        compiler_params=pltpu.CompilerParams(vmem_limit_bytes=28 * 2**20),
        cost_estimate=pl.CostEstimate(
            flops=10 * rows * tokens * channels * channels,
            bytes_accessed=12 * rows * tokens * channels,
            transcendentals=3 * rows * tokens * channels,
        ),
        name="edges",
    )(*in_hbm(pair, gain, bias, w_left, w_right, w_gate))


def product_kernel(both, out, left_turned):
    n_rows, n_cols, _, depth, tokens = both.shape

    def column(col, side):
        return jnp.concatenate([both[row, col, side] for row in range(n_rows)], axis=0)

    for col in range(n_cols):
        left_turned[col * tokens : (col + 1) * tokens, :] = column(col, 0).T
    for col in range(0, n_cols, 2):
        rights = jnp.concatenate([column(col, 1), column(col + 1, 1)], axis=1)
        total = jnp.dot(left_turned[...], rights, preferred_element_type=F32).astype(BF16)
        for part in range(2):
            block = total[:, part * tokens : (part + 1) * tokens]
            out[:, col + part] = block.reshape(n_rows, depth, tokens)


def products(both):
    n_rows, n_cols, _, depth, tokens = both.shape
    size = n_rows * depth
    return pl.pallas_call(
        product_kernel,
        out_shape=jax.ShapeDtypeStruct((n_rows, n_cols, depth, tokens), BF16),
        scratch_shapes=[pltpu.VMEM((size, size), BF16)],
        compiler_params=pltpu.CompilerParams(vmem_limit_bytes=24 * 2**20),
        cost_estimate=pl.CostEstimate(
            flops=2 * size**3, bytes_accessed=6 * size * size, transcendentals=0
        ),
        name="products",
    )(both)


def update_kernel(
    product, gating, gain, bias, weight, out_far, gains, biases, rows_of, out, sems
):
    channels, rows, tokens = product.shape
    pitch = ROWS + PAD
    steps = rows // ROWS
    def send(start):
        place = pl.ds(start, SEND)
        return pltpu.make_async_copy(out.at[place], out_far.at[place], sems.at[start // SEND])

    gains[...] = jnp.broadcast_to(gain[...], (tokens, channels)).T
    biases[...] = jnp.broadcast_to(bias[...], (tokens, channels)).T

    def body(step, carry):
        base = pl.multiple_of(step * ROWS, ROWS)
        for channel in range(channels):
            rows_of[pl.ds(channel * pitch, ROWS), :] = product[
                channel, pl.ds(base, ROWS), :
            ].astype(F32)
        for row in range(ROWS):
            values = rows_of[pl.ds(row, channels, stride=pitch), :]
            center = jnp.sum(values, axis=0, keepdims=True) * (1.0 / channels)
            values = values - center
            spread = jnp.sum(values * values, axis=0, keepdims=True) * (1.0 / channels)
            normed = (values * lax.rsqrt(spread + EPS) * gains[...] + biases[...]).astype(BF16)
            projected = lax.dot_general(
                normed, weight[...], (((0,), (0,)), ((), ())), preferred_element_type=F32
            )
            out[base + row] = gating[base + row] * projected
            if row % SEND == SEND - 1:
                send(base + row + 1 - SEND).start()
        return carry

    lax.fori_loop(0, steps, body, 0, unroll=True)
    for start in range(0, rows, SEND):
        send(start).wait()


def update(product, gating, gain, bias, weight):
    channels, rows, tokens = product.shape
    return pl.pallas_call(
        update_kernel,
        in_specs=[pl.BlockSpec(memory_space=pltpu.VMEM)] * 5,
        out_specs=pl.BlockSpec(memory_space=pltpu.HBM),
        out_shape=jax.ShapeDtypeStruct((rows, tokens, channels), F32),
        scratch_shapes=[
            pltpu.VMEM((channels, tokens), F32),
            pltpu.VMEM((channels, tokens), F32),
            pltpu.VMEM((channels * (ROWS + PAD), tokens), F32),
            pltpu.VMEM((rows, tokens, channels), F32),
            pltpu.SemaphoreType.DMA((rows // SEND,)),
        ],
        compiler_params=pltpu.CompilerParams(vmem_limit_bytes=20 * 2**20),
        cost_estimate=pl.CostEstimate(
            flops=2 * rows * tokens * channels * channels,
            bytes_accessed=10 * rows * tokens * channels,
            transcendentals=0,
        ),
        name="update",
    )(product, gating, gain, bias, weight)


def per_device(n_rows, n_cols, pair, ln_gain, ln_bias, w_left, w_right, w_gate, w_out, out_gain, out_bias):
    rows, tokens, channels = pair.shape
    axes = ("row", "col")
    gain, bias = ln_gain[None], ln_bias[None]
    both, gating = edges(pair, gain, bias, w_left, w_right, w_gate)
    both = lax.all_to_all(both.reshape(channels, 2 * rows, tokens), axes, 0, 0, tiled=True)
    product = products(both.reshape(n_rows, n_cols, 2, rows, tokens)).reshape(channels, rows, tokens)
    product = lax.all_to_all(product, axes, 0, 0, tiled=True)
    return update(product, gating, out_gain[None], out_bias[None], w_out)


def solution(mesh):
    n_rows, n_cols = mesh.shape["row"], mesh.shape["col"]
    return jax.shard_map(
        lambda *args: per_device(n_rows, n_cols, *args),
        mesh=mesh,
        in_specs=(P("row", "col", None), P(), P(), P(), P(), P(), P(), P(), P()),
        out_specs=P("row", "col", None),
        check_vma=False,
    )
```

```python
import jax
import jax.numpy as jnp
from jax import lax
from jax.experimental import pallas as pl
from jax.experimental.pallas import tpu as pltpu
from jax.sharding import PartitionSpec as P

F32, BF16 = jnp.float32, jnp.bfloat16
EPS = 1e-05
FIRST = 16
ROWS = 16
BATCH = 4
SEND = 4
PAD = 4


def in_hbm(*arrays):
    return [pltpu.with_memory_space_constraint(array, pltpu.HBM) for array in arrays]


def edges_kernel(
    pair_far, gain_far, bias_far, left_far, right_far, gate_far, out, gating,
    pair, gain, bias, w_left, w_right, w_gate, weight, left_rows, right_rows, sems,
):
    rows, tokens, channels = pair.shape
    pitch = channels + PAD
    small = [
        pltpu.make_async_copy(far, near, sems.at[place])
        for place, (far, near) in enumerate(
            zip(
                (gain_far, bias_far, left_far, right_far, gate_far),
                (gain, bias, w_left, w_right, w_gate),
            )
        )
    ]

    steps = [(0, FIRST), (FIRST, rows)]
    fetches = [
        pltpu.make_async_copy(
            pair_far.at[pl.ds(start, stop - start)],
            pair.at[pl.ds(start, stop - start)],
            sems.at[5 + step],
        )
        for step, (start, stop) in enumerate(steps)
    ]
    for copy in small[:2]:
        copy.start()
    fetches[0].start()
    for copy in small[2:]:
        copy.start()
    fetches[1].start()
    for copy in small[:2]:
        copy.wait()
    gains = jnp.broadcast_to(gain[...], (BATCH * tokens, channels)).T
    biases = jnp.broadcast_to(bias[...], (BATCH * tokens, channels)).T

    fetches[0].wait()
    for copy in small[2:]:
        copy.wait()
    weight[: 2 * channels] = w_left[...].T * 0.5
    weight[2 * channels :] = w_right[...].T * 0.5
    w_gate[...] = w_gate[...] * 0.5

    for copy, (start, stop) in zip(fetches, steps):
        if start > 0:
            copy.wait()
        for row in range(start, stop, BATCH):
            values = pair[pl.ds(row, BATCH)].reshape(BATCH * tokens, channels).T
            center = jnp.sum(values, axis=0, keepdims=True) * (1.0 / channels)
            values = values - center
            spread = jnp.sum(values * values, axis=0, keepdims=True) * (1.0 / channels)
            normed = (values * lax.rsqrt(spread + EPS) * gains + biases).astype(BF16)
            projected = jnp.dot(weight[...], normed, preferred_element_type=F32)
            gates = lax.dot_general(
                normed, w_gate[...], (((0,), (0,)), ((), ())), preferred_element_type=F32
            )
            gating[pl.ds(row, BATCH)] = 0.5 * jnp.tanh(gates).reshape(BATCH, tokens, channels) + 0.5
            gate_left, left, gate_right, right = jnp.split(projected, 4, axis=0)
            lefts = (jnp.tanh(gate_left) + 1.0) * left
            rights = (jnp.tanh(gate_right) + 1.0) * right
            for part in range(BATCH):
                place = pl.ds((row + part) * pitch, channels)
                lanes = slice(part * tokens, (part + 1) * tokens)
                left_rows[place, :] = lefts[:, lanes]
                right_rows[place, :] = rights[:, lanes]
        for channel in range(channels):
            place = pl.ds(start * pitch + channel, stop - start, stride=pitch)
            out[channel, 0, start:stop, :] = left_rows[place, :].astype(BF16)
            out[channel, 1, start:stop, :] = right_rows[place, :].astype(BF16)


def edges(pair, gain, bias, w_left, w_right, w_gate):
    rows, tokens, channels = pair.shape
    far = pl.BlockSpec(memory_space=pltpu.HBM)
    return pl.pallas_call(
        edges_kernel,
        in_specs=[far] * 6,
        out_specs=[pl.BlockSpec(memory_space=pltpu.VMEM)] * 2,
        out_shape=[
            jax.ShapeDtypeStruct((channels, 2, rows, tokens), BF16),
            jax.ShapeDtypeStruct(pair.shape, F32),
        ],
        scratch_shapes=[
            pltpu.VMEM(pair.shape, F32),
            pltpu.VMEM(gain.shape, F32),
            pltpu.VMEM(bias.shape, F32),
            pltpu.VMEM(w_left.shape, BF16),
            pltpu.VMEM(w_right.shape, BF16),
            pltpu.VMEM(w_gate.shape, BF16),
            pltpu.VMEM((4 * channels, channels), BF16),
            pltpu.VMEM((rows * (channels + PAD), tokens), F32),
            pltpu.VMEM((rows * (channels + PAD), tokens), F32),
            pltpu.SemaphoreType.DMA((7,)),
        ],
        compiler_params=pltpu.CompilerParams(vmem_limit_bytes=28 * 2**20),
        cost_estimate=pl.CostEstimate(
            flops=10 * rows * tokens * channels * channels,
            bytes_accessed=12 * rows * tokens * channels,
            transcendentals=3 * rows * tokens * channels,
        ),
        name="edges",
    )(*in_hbm(pair, gain, bias, w_left, w_right, w_gate))


def product_kernel(both, out, left_turned):
    n_rows, n_cols, _, depth, tokens = both.shape

    def column(col, side):
        return jnp.concatenate([both[row, col, side] for row in range(n_rows)], axis=0)

    for col in range(n_cols):
        left_turned[col * tokens : (col + 1) * tokens, :] = column(col, 0).T
    for col in range(0, n_cols, 2):
        rights = jnp.concatenate([column(col, 1), column(col + 1, 1)], axis=1)
        total = jnp.dot(left_turned[...], rights, preferred_element_type=F32).astype(BF16)
        for part in range(2):
            block = total[:, part * tokens : (part + 1) * tokens]
            out[:, col + part] = block.reshape(n_rows, depth, tokens)


def products(both):
    n_rows, n_cols, _, depth, tokens = both.shape
    size = n_rows * depth
    return pl.pallas_call(
        product_kernel,
        out_shape=jax.ShapeDtypeStruct((n_rows, n_cols, depth, tokens), BF16),
        scratch_shapes=[pltpu.VMEM((size, size), BF16)],
        compiler_params=pltpu.CompilerParams(vmem_limit_bytes=24 * 2**20),
        cost_estimate=pl.CostEstimate(
            flops=2 * size**3, bytes_accessed=6 * size * size, transcendentals=0
        ),
        name="products",
    )(both)


def update_kernel(
    product, gating, gain, bias, weight, out_far, gains, biases, rows_of, out, sems
):
    channels, rows, tokens = product.shape
    pitch = ROWS + PAD
    steps = rows // ROWS
    def send(start):
        place = pl.ds(start, SEND)
        return pltpu.make_async_copy(out.at[place], out_far.at[place], sems.at[start // SEND])

    gains[...] = jnp.broadcast_to(gain[...], (tokens, channels)).T
    biases[...] = jnp.broadcast_to(bias[...], (tokens, channels)).T

    def body(step, carry):
        base = pl.multiple_of(step * ROWS, ROWS)
        for channel in range(channels):
            rows_of[pl.ds(channel * pitch, ROWS), :] = product[
                channel, pl.ds(base, ROWS), :
            ].astype(F32)
        for row in range(ROWS):
            values = rows_of[pl.ds(row, channels, stride=pitch), :]
            center = jnp.sum(values, axis=0, keepdims=True) * (1.0 / channels)
            values = values - center
            spread = jnp.sum(values * values, axis=0, keepdims=True) * (1.0 / channels)
            normed = (values * lax.rsqrt(spread + EPS) * gains[...] + biases[...]).astype(BF16)
            projected = lax.dot_general(
                normed, weight[...], (((0,), (0,)), ((), ())), preferred_element_type=F32
            )
            out[base + row] = gating[base + row] * projected
            if row % SEND == SEND - 1:
                send(base + row + 1 - SEND).start()
        return carry

    lax.fori_loop(0, steps, body, 0, unroll=True)
    for start in range(0, rows, SEND):
        send(start).wait()


def update(product, gating, gain, bias, weight):
    channels, rows, tokens = product.shape
    return pl.pallas_call(
        update_kernel,
        in_specs=[pl.BlockSpec(memory_space=pltpu.VMEM)] * 5,
        out_specs=pl.BlockSpec(memory_space=pltpu.HBM),
        out_shape=jax.ShapeDtypeStruct((rows, tokens, channels), F32),
        scratch_shapes=[
            pltpu.VMEM((channels, tokens), F32),
            pltpu.VMEM((channels, tokens), F32),
            pltpu.VMEM((channels * (ROWS + PAD), tokens), F32),
            pltpu.VMEM((rows, tokens, channels), F32),
            pltpu.SemaphoreType.DMA((rows // SEND,)),
        ],
        compiler_params=pltpu.CompilerParams(vmem_limit_bytes=20 * 2**20),
        cost_estimate=pl.CostEstimate(
            flops=2 * rows * tokens * channels * channels,
            bytes_accessed=10 * rows * tokens * channels,
            transcendentals=0,
        ),
        name="update",
    )(product, gating, gain, bias, weight)


def per_device(n_rows, n_cols, pair, ln_gain, ln_bias, w_left, w_right, w_gate, w_out, out_gain, out_bias):
    rows, tokens, channels = pair.shape
    axes = ("row", "col")
    gain, bias = ln_gain[None], ln_bias[None]
    both, gating = edges(pair, gain, bias, w_left, w_right, w_gate)
    both = lax.all_to_all(both.reshape(channels, 2 * rows, tokens), axes, 0, 0, tiled=True)
    product = products(both.reshape(n_rows, n_cols, 2, rows, tokens)).reshape(channels, rows, tokens)
    product = lax.all_to_all(product, axes, 0, 0, tiled=True)
    return update(product, gating, out_gain[None], out_bias[None], w_out)


def solution(mesh):
    n_rows, n_cols = mesh.shape["row"], mesh.shape["col"]
    return jax.shard_map(
        lambda *args: per_device(n_rows, n_cols, *args),
        mesh=mesh,
        in_specs=(P("row", "col", None), P(), P(), P(), P(), P(), P(), P(), P()),
        out_specs=P("row", "col", None),
        check_vma=False,
    )
```
